256 devices in a mesh: wide: 32 (over x, y, core), narrow: 8 (over z).
Axes of the slice: x: 4, y: 4, z: 8, core: 2. Of those that a mesh axis runs over, the one named last changes fastest.
Arguments:
- test_matrix: bfloat16 [64, 1048576], P(None, ('wide', 'narrow')), may hold values from -6 to 6
- weights: bfloat16 [8192, 8, 128, 128], P(('wide', 'narrow'))
- block_cols: int32 [8192, 8], P(('wide', 'narrow')), may hold values from 0 to 49, as said below
- export_rows: int32 [256, 2], replicated, may hold values from 0 to 31, as said below
- row_count: int32 [256], P(('wide', 'narrow')), may hold values from 1024 to 4096, as said below
Outputs:
- range_basis: float32 [64, 1048576], P(None, ('wide', 'narrow'))
The draws below stay inside these ranges and needn't reach their ends.
Inputs may be any that keep to these rules, and one draw needn't show every extreme that they name: `block_cols`: an entry below 32 names a block row of the same part; an entry c0 of 32 or more names entry (c0 - 32) % 2 of the export list of the neighbouring part at position h = (c0 - 32) // 2 as in the reference program; h is never 4; slot 0 of block row p * 32 + r is always r, the row's own block. `export_rows`: the 2 entries of one part are distinct. The present nodes of a part are its first row_count node slots.
All inputs are finite; a program needn't handle non-finite values.
Results may differ from the reference program's by a relative error of at most 0.0041.
Values may be sent and summed in bfloat16 or wider, within the bound.
No kernel may reach another device: no remote copies, remote signals or barrier semaphores. Data moves between devices by JAX's collectives and lax.ppermute only.
A program may use at most 64 MiB of HBM per device.

```python
import math
import jax
import jax.numpy as jnp
from jax import lax

K = 64
BS = 128
NB = 8
EB = 2
RB = 32
ROWS_DEV = 4096
BLOCKS = 8192
NODES = 1048576
N_WIDE = 32
N_NARROW = 8
DEVICES = 256


def draw_weights(key, part):
    key = jax.random.fold_in(key, 31)
    subkeys = jax.random.split(key, 2)
    base = jax.random.normal(subkeys[0], (BLOCKS, NB, BS, BS), jnp.float32)
    scales = jnp.exp(jax.random.uniform(subkeys[1], (BLOCKS, 1, BS, 1), jnp.float32, 0.0, 2.3))
    identity = jnp.eye(BS, dtype=jnp.float32)
    slot_mark = (jnp.arange(NB) == 0).astype(jnp.float32)
    diagonal = 3.0 * slot_mark[None, :, None, None] * identity[None, None, :, :]
    return ((base / (NB * BS) ** 0.5 + diagonal) * scales).astype(jnp.bfloat16)


def draw_block_cols(key, part):
    key = jax.random.fold_in(key, 32)
    subkeys = jax.random.split(key, 4)
    local_cols = jax.random.randint(subkeys[0], (BLOCKS, NB), 0, RB)
    neighbour_draw = jax.random.randint(subkeys[1], (BLOCKS, NB), 0, 8)
    neighbour_spot = neighbour_draw + (neighbour_draw >= 4).astype(jnp.int32)
    export_entry = jax.random.randint(subkeys[2], (BLOCKS, NB), 0, EB)
    halo_cols = RB + neighbour_spot * EB + export_entry
    choose_local = jax.random.randint(subkeys[3], (BLOCKS, NB), 0, 4) < 3
    result = jnp.where(choose_local, local_cols, halo_cols)
    own_block = jnp.arange(BLOCKS, dtype=jnp.int32) % RB
    result = result.at[:, 0].set(own_block)
    result = result.at[0, NB - 1].set(RB + 9 * EB - 1)
    return result.astype(jnp.int32)


def draw_export_rows(key, part):
    key = jax.random.fold_in(key, 33)
    subkeys = jax.random.split(key, DEVICES)
    orders = jax.vmap(lambda single: jax.random.permutation(single, RB))(subkeys)
    return orders[:, :EB].astype(jnp.int32)


def draw_row_count(key, part):
    key = jax.random.fold_in(key, 34)
    subkeys = jax.random.split(key, 4)
    divisor = jax.random.randint(subkeys[0], (DEVICES,), 1, 3)
    highest = ROWS_DEV // divisor
    counts = highest - jax.random.randint(subkeys[1], (DEVICES,), 0, highest // 2 + 1)
    fullest = jax.random.randint(subkeys[2], (), 0, DEVICES)
    emptiest = (fullest + 1 + jax.random.randint(subkeys[3], (), 0, DEVICES - 1)) % DEVICES
    counts = counts.at[fullest].set(ROWS_DEV).at[emptiest].set(ROWS_DEV // 4)
    return counts.astype(jnp.int32)


def block_scale(own_key, dims, cuts, smallest, top_value):
    level, own = 1.0, jax.random.fold_in(own_key, 6)
    for position, parts in cuts:
        heights = jnp.exp(jax.random.uniform(jax.random.fold_in(own, position), (parts,), jnp.float32, smallest / len(cuts), top_value / len(cuts)))
        level = level * jnp.repeat(heights, dims[position] // parts).reshape([-1 if axis == position else 1 for axis in range(len(dims))])
    return level


def centred(key, shape, spread, limit, cuts=(), kind=jnp.bfloat16):
    loudness = block_scale(key, shape, cuts, -0.22, 0.18) if cuts else 1.0
    drawn = jax.random.normal(key, shape, jnp.float32) * spread * loudness
    return jnp.minimum(jnp.maximum(drawn, -limit), limit).astype(kind)


def setup_inputs(seed: int = 0) -> dict:
    key_list = jax.random.split(jax.random.key(seed), 6)
    test_matrix = centred(key_list[0], (K, NODES), 1.0, 6.0, ((1, 256),))
    weights = draw_weights(jax.random.fold_in(key_list[5], 71), 0)
    block_cols = draw_block_cols(jax.random.fold_in(key_list[5], 71), 0)
    export_rows = draw_export_rows(jax.random.fold_in(key_list[5], 71), 0)
    row_count = draw_row_count(jax.random.fold_in(key_list[5], 71), 0)
    return dict(test_matrix=test_matrix, weights=weights, block_cols=block_cols, export_rows=export_rows, row_count=row_count)


EPSILON = 1e-06

def part_degree(part_weights):
    return lax.optimization_barrier(jnp.sum(jnp.abs(part_weights.astype(jnp.float32)), axis=(1, 3))) + EPSILON

def global_slots(block_cols, export_rows):
    slot_cols = block_cols.reshape(DEVICES, RB, NB).astype(jnp.int32)
    part_ids = jnp.arange(DEVICES, dtype=jnp.int32)[:, None, None]
    wide_pos = part_ids // N_NARROW
    narrow_pos = part_ids % N_NARROW
    offset = jnp.maximum(slot_cols - RB, 0)
    neighbour_spot = offset // EB
    export_entry = offset % EB
    neighbour = (wide_pos + neighbour_spot // 3 - 1) % N_WIDE * N_NARROW + (narrow_pos + neighbour_spot % 3 - 1) % N_NARROW
    remote = neighbour * RB + export_rows[neighbour, export_entry].astype(jnp.int32)
    return jnp.where(slot_cols < RB, part_ids * RB + slot_cols, remote).astype(jnp.int32)

def apply_blocks(block_table, slot_ids, weights):
    part_weights = weights.reshape(DEVICES, RB, NB, BS, BS)

    def one_part(pieces):
        part_slots, part_block = pieces
        gathered = jnp.take(block_table, part_slots, axis=1).astype(jnp.float32)
        return jnp.einsum('krsc,rsic->kri', gathered, part_block.astype(jnp.float32))
    result = lax.map(one_part, (slot_ids, part_weights))
    return jnp.transpose(result, (1, 0, 2, 3))

def reference(test_matrix, weights, block_cols, export_rows, row_count):
    degree = lax.map(part_degree, weights.reshape(DEVICES, RB, NB, BS, BS))
    positions = jnp.arange(ROWS_DEV, dtype=jnp.int32).reshape(RB, BS)
    live_rows = (positions[None] < row_count.astype(jnp.int32)[:, None, None]).astype(jnp.float32)
    inverse_root = lax.rsqrt(degree)
    slot_ids = global_slots(block_cols, export_rows)
    probe = test_matrix.reshape(K, DEVICES, RB, BS).astype(jnp.float32)
    first_input = (probe * inverse_root * live_rows).astype(jnp.bfloat16)
    first_out = apply_blocks(first_input.reshape(K, BLOCKS, BS), slot_ids, weights)
    second_input = (first_out / degree * live_rows).astype(jnp.bfloat16)
    second_out = apply_blocks(second_input.reshape(K, BLOCKS, BS), slot_ids, weights)
    sketch = (second_out * inverse_root * live_rows).reshape(K, NODES)
    gram = jnp.dot(sketch, sketch.T, precision=lax.Precision.HIGHEST)
    lower_factor = jnp.linalg.cholesky(gram)
    solved = jax.scipy.linalg.solve_triangular(lower_factor, sketch, lower=True)
    return solved * math.sqrt(NODES)
```

```python
import math

import jax
import jax.numpy as jnp
from jax import lax
from jax.sharding import PartitionSpec as P

EPSILON = 1e-06
AXES = ("wide", "narrow")


def shifted(value, axis, step):
    count = lax.axis_size(axis)
    return lax.ppermute(value, axis, [(i, (i + step) % count) for i in range(count)])


def swapped(value, axis, partner):
    return lax.ppermute(value, axis, [(i, partner(i)) for i in range(lax.axis_size(axis))])


def halo_blocks(exports):
    count = lax.axis_size("wide")
    column = jnp.concatenate([shifted(exports, "narrow", 1), exports, shifted(exports, "narrow", -1)], axis=0)
    chip = swapped(column, "wide", lambda i: i ^ 1)
    other = swapped(column, "wide", lambda i: (i + 1) % count if i % 2 else (i - 1) % count)
    return jnp.concatenate([column, chip, other], axis=0)


def summed(value):
    wide_steps = [lambda i: i ^ 1, lambda i: i ^ 2, lambda i: i ^ 6, lambda i: i ^ 8, lambda i: i ^ 24]
    for step in wide_steps:
        value = value + swapped(value, "wide", step)
    for step in [lambda i: i ^ 1, lambda i: i ^ 3]:
        value = value + swapped(value, "narrow", step)
    return value + swapped(value, "narrow", lambda i: (i + 2 if i % 4 >= 2 else i - 2) % 8)


def local(test_matrix, weights, block_cols, export_rows, row_count):
    row_blocks = weights.shape[0]
    block_size = weights.shape[2]
    columns = test_matrix.shape[0]
    exports_each = export_rows.shape[1]
    degree = jnp.sum(jnp.abs(weights), axis=(1, 3), dtype=jnp.float32) + EPSILON
    positions = jnp.arange(row_blocks * block_size, dtype=jnp.int32).reshape(row_blocks, block_size)
    live_rows = (positions < row_count[0]).astype(jnp.float32)
    inverse_root = lax.rsqrt(degree)
    wide_pos = lax.axis_index("wide")
    part = wide_pos * lax.axis_size("narrow") + lax.axis_index("narrow")
    own_exports = lax.dynamic_index_in_dim(export_rows, part, 0, keepdims=False)
    group = 3 * exports_each
    offset = jnp.maximum(block_cols - row_blocks, 0)
    wide_spot = offset // group
    on_chip = (wide_spot == 2) == (wide_pos % 2 == 0)
    source = jnp.where(wide_spot == 1, 0, jnp.where(on_chip, 1, 2))
    slot_index = jnp.where(block_cols < row_blocks, block_cols, row_blocks + source * group + offset % group)

    def apply_blocks(vectors):
        exports = jnp.take(vectors, own_exports, axis=0)
        block_table = jnp.concatenate([vectors, halo_blocks(exports)], axis=0)
        gathered = jnp.take(block_table, slot_index, axis=0)
        return jnp.einsum("rskc,rsic->rki", gathered, weights, preferred_element_type=jnp.float32)

    probe = test_matrix.reshape(columns, row_blocks, block_size).transpose(1, 0, 2)
    first_input = (probe * (inverse_root * live_rows)[:, None]).astype(jnp.bfloat16)
    first_out = apply_blocks(first_input)
    second_input = (first_out / degree[:, None] * live_rows[:, None]).astype(jnp.bfloat16)
    second_out = apply_blocks(second_input)
    sketch = second_out * (inverse_root * live_rows)[:, None]
    sketch = sketch.transpose(1, 0, 2).reshape(columns, row_blocks * block_size)
    gram = summed(jnp.dot(sketch, sketch.T, precision=lax.Precision.HIGHEST))
    lower_factor = jnp.linalg.cholesky(gram)
    node_total = lax.axis_size(AXES) * row_blocks * block_size
    solved = jax.scipy.linalg.solve_triangular(lower_factor, sketch, lower=True)
    return solved * math.sqrt(node_total)


def solution(mesh):
    in_specs = (
        P(None, AXES),
        P(AXES, None, None, None),
        P(AXES, None),
        P(),
        P(AXES),
    )
    return jax.shard_map(local, mesh=mesh, in_specs=in_specs, out_specs=P(None, AXES), check_vma=False)
```

```python
import functools
import math

import jax
import jax.numpy as jnp
from jax import lax
from jax.experimental import pallas as pl
from jax.experimental.pallas import tpu as pltpu
from jax.sharding import PartitionSpec as P

EPSILON = 1e-06
AXES = ("wide", "narrow")
ROWS_STEP = 8
VMEM = pl.BlockSpec(memory_space=pltpu.VMEM)
LIMIT = 24 * 1024 * 1024
LAST = (((1,), (1,)), ((), ()))


def lanes(blocks):
    return jnp.concatenate([blocks[i] for i in range(blocks.shape[0])], axis=1)


def block_degree(blocks):
    ones = jnp.ones((8, blocks.shape[0] * blocks.shape[2]), blocks.dtype)
    sums = lax.dot_general(ones, lanes(jnp.abs(blocks)), LAST, preferred_element_type=jnp.float32)
    return sums[0:1] + EPSILON


def live_mask(row, block_size, present):
    position = lax.broadcasted_iota(jnp.int32, (1, block_size), 1) + row * block_size
    return (position < present).astype(jnp.float32)


def scaled(probe, degree, live):
    return (probe.astype(jnp.float32) * lax.rsqrt(degree) * live).astype(jnp.bfloat16)


def export_first_kernel(exports, count, probe, weights, out):
    row = exports[pl.program_id(0)]
    live = live_mask(row, probe.shape[1], count[0])
    out[0] = scaled(probe[...], block_degree(weights[0]), live)


def first_kernel(count, probe, weights, degree_out, out):
    step, rows = pl.program_id(0), weights.shape[0]
    size = weights.shape[2]
    for i in range(rows):
        degree = block_degree(weights[i])
        degree_out[i : i + 1, :] = degree
        live = live_mask(step * rows + i, size, count[0])
        out[i] = scaled(probe[:, i * size : (i + 1) * size], degree, live)


def fill_table(table, parts):
    start = 0
    for part in parts:
        table[start : start + part.shape[0]] = part[...]
        start += part.shape[0]


def applied(table, slots, row, blocks):
    vectors = jnp.concatenate([table[slots[row, s]] for s in range(blocks.shape[0])], axis=1)
    return lax.dot_general(vectors, lanes(blocks), LAST, preferred_element_type=jnp.float32)


def export_second_kernel(exports, count, slots, own, column, chip, other, degree, weights, out, table):
    @pl.when(pl.program_id(0) == 0)
    def _():
        fill_table(table, (own, column, chip, other))

    row = exports[pl.program_id(0)]
    live = live_mask(row, weights.shape[2], count[0])
    product = applied(table, slots, row, weights[0])
    out[0] = (product / degree[pl.ds(row, 1), :] * live).astype(jnp.bfloat16)


def second_kernel(count, slots, own, column, chip, other, degree, weights, out, table):
    step, rows = pl.program_id(0), weights.shape[0]

    @pl.when(step == 0)
    def _():
        fill_table(table, (own, column, chip, other))

    for i in range(rows):
        row = step * rows + i
        live = live_mask(row, weights.shape[2], count[0])
        product = applied(table, slots, row, weights[i])
        out[i] = (product / degree[i : i + 1, :] * live).astype(jnp.bfloat16)


def halves(value):
    high = value.astype(jnp.bfloat16)
    return high, (value - high.astype(jnp.float32)).astype(jnp.bfloat16)


def sketch_kernel(count, slots, own, column, chip, other, degree, weights, sketch, gram, table, main, cross):
    step, rows = pl.program_id(0), weights.shape[0]
    size = weights.shape[2]

    @pl.when(step == 0)
    def _():
        fill_table(table, (own, column, chip, other))
        main[...] = jnp.zeros_like(main)
        cross[...] = jnp.zeros_like(cross)

    for i in range(rows):
        row = step * rows + i
        live = live_mask(row, size, count[0])
        product = applied(table, slots, row, weights[i])
        sketch[:, i * size : (i + 1) * size] = product * lax.rsqrt(degree[i : i + 1, :]) * live
    high, low = halves(sketch[...])
    main[...] += lax.dot_general(high, high, LAST, preferred_element_type=jnp.float32)
    cross[...] += lax.dot_general(high, low, LAST, preferred_element_type=jnp.float32)

    @pl.when(step == pl.num_programs(0) - 1)
    def _():
        total = main[...] + cross[...] + cross[...].T
        half = total.shape[0] // 2
        gram[...] = jnp.concatenate([total[:half], total[half:]], axis=1)


def factor_kernel(scale, grams, sketch, out, inverse):
    packed = grams[0]
    for i in range(1, grams.shape[0]):
        packed = packed + grams[i]
    half = packed.shape[0]
    count = 2 * half
    total = jnp.concatenate([packed[:, :count], packed[:, count:]], axis=0)
    identity = (
        lax.broadcasted_iota(jnp.int32, (count, count), 0) == lax.broadcasted_iota(jnp.int32, (count, count), 1)
    ).astype(jnp.float32)
    rest = jnp.concatenate([identity, total], axis=1)
    width = 8
    for start in range(0, count, width):
        height = rest.shape[0]
        sides = [
            jnp.broadcast_to(rest[:, count + start + j : count + start + j + 1], rest.shape) for j in range(width)
        ]
        below = lax.broadcasted_iota(jnp.int32, rest.shape, 0)
        for j in range(width):
            pivot = sides[j][j : j + 1, :]
            factors = jnp.where(below > j, sides[j] * (1.0 / pivot), 0.0)
            line = rest[j : j + 1, :]
            inverse[start + j : start + j + 1, :] = line * (lax.rsqrt(pivot) * scale)
            rest = rest - factors * line
            for k in range(j + 1, width):
                sides[k] = sides[k] - factors * sides[k][j : j + 1, :]
        if start + width < count:
            rest = rest[width:, :]
    high, low = halves(inverse[:, :count])
    value_high, value_low = halves(sketch[...])
    out[...] = (
        jnp.dot(high, value_high, preferred_element_type=jnp.float32)
        + jnp.dot(high, value_low, preferred_element_type=jnp.float32)
        + jnp.dot(low, value_high, preferred_element_type=jnp.float32)
    )


def cost(flops, moved):
    return pl.CostEstimate(flops=flops, bytes_accessed=moved, transcendentals=0)


def call(kernel, prefetch, grid, in_specs, out_specs, out_shape, scratch, flops, moved):
    return pl.pallas_call(
        kernel,
        grid_spec=pltpu.PrefetchScalarGridSpec(
            num_scalar_prefetch=prefetch, grid=grid, in_specs=in_specs, out_specs=out_specs, scratch_shapes=scratch
        ),
        out_shape=out_shape,
        compiler_params=pltpu.CompilerParams(vmem_limit_bytes=LIMIT, dimension_semantics=("arbitrary",) * len(grid)),
        cost_estimate=cost(flops, moved),
    )


def whole(shape):
    return pl.BlockSpec(shape, lambda *_: (0,) * len(shape))


class Kernels:
    def __init__(self, columns, row_blocks, slots, size, exports, halo):
        self.k, self.rb, self.nb, self.bs, self.eb = columns, row_blocks, slots, size, exports
        self.halo = halo
        self.step = min(ROWS_STEP, row_blocks)
        self.bytes_weights = row_blocks * slots * size * size * 2
        self.flops = 2 * columns * row_blocks * slots * size * size
        self.tables = [whole((row_blocks, columns, size))] + [whole((halo // 3, columns, size))] * 3
        self.table = pltpu.VMEM((row_blocks + halo, columns, size), jnp.bfloat16)

    def weights(self):
        return pl.BlockSpec((self.step, self.nb, self.bs, self.bs), lambda i, *_: (i, 0, 0, 0))

    def one_weights(self):
        return pl.BlockSpec((1, self.nb, self.bs, self.bs), lambda i, exports, *_: (exports[i], 0, 0, 0))

    def export_first(self, exports, count, probe, weights):
        return call(
            export_first_kernel,
            2,
            (self.eb,),
            [pl.BlockSpec((self.k, self.bs), lambda i, exports, *_: (0, exports[i])), self.one_weights()],
            pl.BlockSpec((1, self.k, self.bs), lambda i, *_: (i, 0, 0)),
            jax.ShapeDtypeStruct((self.eb, self.k, self.bs), jnp.bfloat16),
            [],
            self.flops // 16,
            self.bytes_weights // 16,
        )(exports, count, probe, weights)

    def first(self, count, probe, weights):
        return call(
            first_kernel,
            1,
            (self.rb // self.step,),
            [pl.BlockSpec((self.k, self.step * self.bs), lambda i, *_: (0, i)), self.weights()],
            [
                pl.BlockSpec((self.step, self.bs), lambda i, *_: (i, 0)),
                pl.BlockSpec((self.step, self.k, self.bs), lambda i, *_: (i, 0, 0)),
            ],
            [
                jax.ShapeDtypeStruct((self.rb, self.bs), jnp.float32),
                jax.ShapeDtypeStruct((self.rb, self.k, self.bs), jnp.bfloat16),
            ],
            [],
            self.flops,
            self.bytes_weights,
        )(count, probe, weights)

    def export_second(self, exports, count, slots, tables, degree, weights):
        return call(
            export_second_kernel,
            3,
            (self.eb,),
            self.tables + [whole((self.rb, self.bs)), self.one_weights()],
            pl.BlockSpec((1, self.k, self.bs), lambda i, *_: (i, 0, 0)),
            jax.ShapeDtypeStruct((self.eb, self.k, self.bs), jnp.bfloat16),
            [self.table],
            self.flops // 16,
            self.bytes_weights // 16,
        )(exports, count, slots, *tables, degree, weights)

    def second(self, count, slots, tables, degree, weights):
        return call(
            second_kernel,
            2,
            (self.rb // self.step,),
            self.tables + [pl.BlockSpec((self.step, self.bs), lambda i, *_: (i, 0)), self.weights()],
            pl.BlockSpec((self.step, self.k, self.bs), lambda i, *_: (i, 0, 0)),
            jax.ShapeDtypeStruct((self.rb, self.k, self.bs), jnp.bfloat16),
            [self.table],
            self.flops,
            self.bytes_weights,
        )(count, slots, *tables, degree, weights)

    def sketch(self, count, slots, tables, degree, weights):
        k = self.k
        return call(
            sketch_kernel,
            2,
            (self.rb // self.step,),
            self.tables + [pl.BlockSpec((self.step, self.bs), lambda i, *_: (i, 0)), self.weights()],
            [pl.BlockSpec((k, self.step * self.bs), lambda i, *_: (0, i)), whole((k // 2, 2 * k))],
            [
                jax.ShapeDtypeStruct((k, self.rb * self.bs), jnp.float32),
                jax.ShapeDtypeStruct((k // 2, 2 * k), jnp.float32),
            ],
            [self.table, pltpu.VMEM((k, k), jnp.float32), pltpu.VMEM((k, k), jnp.float32)],
            self.flops,
            self.bytes_weights,
        )(count, slots, *tables, degree, weights)

    def factor(self, scale, grams, sketch):
        return pl.pallas_call(
            functools.partial(factor_kernel, scale),
            in_specs=[VMEM, VMEM],
            out_specs=VMEM,
            out_shape=jax.ShapeDtypeStruct(sketch.shape, jnp.float32),
            scratch_shapes=[pltpu.VMEM((self.k, 2 * self.k), jnp.float32)],
            compiler_params=pltpu.CompilerParams(vmem_limit_bytes=LIMIT),
            cost_estimate=cost(6 * self.k * sketch.size, 8 * sketch.size),
        )(grams, sketch)


def shifted(value, axis, step):
    count = lax.axis_size(axis)
    return lax.ppermute(value, axis, [(i, (i + step) % count) for i in range(count)])


def swapped(value, axis, partner):
    return lax.ppermute(value, axis, [(i, partner(i)) for i in range(lax.axis_size(axis))])


def halo_blocks(exports):
    count = lax.axis_size("wide")
    column = jnp.concatenate([shifted(exports, "narrow", 1), exports, shifted(exports, "narrow", -1)], axis=0)
    chip = swapped(column, "wide", lambda i: i ^ 1)
    other = swapped(column, "wide", lambda i: (i + 1) % count if i % 2 else (i - 1) % count)
    return column, chip, other


def from_all(value, axis, groups=None):
    count = len(groups[0]) if groups else lax.axis_size(axis)
    copies = jnp.broadcast_to(value[None], (count, *value.shape))
    return lax.all_to_all(copies, axis, 0, 0, axis_index_groups=groups, tiled=True)


def gathered_grams(gram):
    chip = gram + swapped(gram, "wide", lambda i: i ^ 1)
    count = lax.axis_size("wide")
    groups = [list(range(core, count, 2)) for core in range(2)]
    return from_all(jnp.sum(from_all(chip, "wide", groups), axis=0), "narrow")


def local(test_matrix, weights, block_cols, export_rows, row_count):
    row_blocks, slots, size, _ = weights.shape
    columns, exports_each = test_matrix.shape[0], export_rows.shape[1]
    group = 3 * exports_each
    kernels = Kernels(columns, row_blocks, slots, size, exports_each, 3 * group)

    wide_pos = lax.axis_index("wide")
    part = wide_pos * lax.axis_size("narrow") + lax.axis_index("narrow")
    own_exports = lax.dynamic_index_in_dim(export_rows, part, 0, keepdims=False)
    offset = jnp.maximum(block_cols - row_blocks, 0)
    wide_spot = offset // group
    on_chip = (wide_spot == 2) == (wide_pos % 2 == 0)
    source = jnp.where(wide_spot == 1, 0, jnp.where(on_chip, 1, 2))
    slot_index = jnp.where(block_cols < row_blocks, block_cols, row_blocks + source * group + offset % group)

    first_exports = kernels.export_first(own_exports, row_count, test_matrix, weights)
    first_halo = halo_blocks(first_exports)
    degree, first_input = kernels.first(row_count, test_matrix, weights)
    tables = (first_input, *first_halo)
    second_exports = kernels.export_second(own_exports, row_count, slot_index, tables, degree, weights)
    second_halo = halo_blocks(second_exports)
    second_input = kernels.second(row_count, slot_index, tables, degree, weights)
    sketch, gram = kernels.sketch(row_count, slot_index, (second_input, *second_halo), degree, weights)
    grams = gathered_grams(gram)
    node_total = lax.axis_size(AXES) * row_blocks * size
    return kernels.factor(math.sqrt(node_total), grams, sketch)


def solution(mesh):
    in_specs = (
        P(None, AXES),
        P(AXES, None, None, None),
        P(AXES, None),
        P(),
        P(AXES),
    )
    return jax.shard_map(local, mesh=mesh, in_specs=in_specs, out_specs=P(None, AXES), check_vma=False)
```

```python
import functools
import math

import jax
import jax.numpy as jnp
from jax import lax
from jax.experimental import pallas as pl
from jax.experimental.pallas import tpu as pltpu
from jax.sharding import PartitionSpec as P

EPSILON = 1e-06
AXES = ("wide", "narrow")
ROWS_STEP = 8
VMEM = pl.BlockSpec(memory_space=pltpu.VMEM)
LIMIT = 24 * 1024 * 1024
LAST = (((1,), (1,)), ((), ()))


def lanes(blocks):
    return jnp.concatenate([blocks[i] for i in range(blocks.shape[0])], axis=1)


def block_degree(blocks):
    ones = jnp.ones((8, blocks.shape[0] * blocks.shape[2]), blocks.dtype)
    sums = lax.dot_general(ones, lanes(jnp.abs(blocks)), LAST, preferred_element_type=jnp.float32)
    return sums[0:1] + EPSILON


def live_mask(row, block_size, present):
    position = lax.broadcasted_iota(jnp.int32, (1, block_size), 1) + row * block_size
    return (position < present).astype(jnp.float32)


def scaled(probe, degree, live):
    return (probe.astype(jnp.float32) * lax.rsqrt(degree) * live).astype(jnp.bfloat16)


def export_first_kernel(
    exports, count, probe, weights, out, probe_here, weights_here, probe_sems, weights_sems
):
    pieces = weights_sems.shape[1]
    slots, size = weights.shape[1] // pieces, weights.shape[2]
    rows = [exports[i] for i in range(exports.shape[0])]
    copies = []
    for i, row in enumerate(rows):
        start = pl.multiple_of(row * size, size)
        copies.append(pltpu.make_async_copy(probe.at[:, pl.ds(start, size)], probe_here.at[i], probe_sems.at[i]))
        for j in range(pieces):
            some = pl.ds(j * slots, slots)
            copies.append(
                pltpu.make_async_copy(weights.at[row, some], weights_here.at[i, some], weights_sems.at[i, j])
            )
    for copy in copies:
        copy.start()
    for copy in copies:
        copy.wait()
    for i, row in enumerate(rows):
        live = live_mask(row, size, count[0])
        out[i] = scaled(probe_here[i], block_degree(weights_here[i]), live)


def first_kernel(count, probe, weights, passed, degree_out, live_out, out, passed_out):
    rows, size = weights.shape[0], weights.shape[2]
    passed_out[...] = passed[...]

    @pl.loop(0, rows // ROWS_STEP)
    def _(step):
        for i in range(ROWS_STEP):
            row = step * ROWS_STEP + i
            degree = block_degree(weights[row])
            degree_out[pl.ds(row, 1), :] = degree
            live = live_mask(row, size, count[0])
            live_out[pl.ds(row, 1), :] = live
            out[row] = scaled(probe[:, pl.ds(pl.multiple_of(row * size, size), size)], degree, live)


def fill_table(table, owns, column, chip, other):
    start = 0
    for own in owns:
        table[start : start + own.shape[0]] = own[...]
        start += own.shape[0]
    group = column.shape[0]
    odd = lax.axis_index("wide") & 1
    table[start + group : start + 2 * group] = column[...]
    table[pl.ds(start + 2 * group * (1 - odd), group)] = chip[...]
    table[pl.ds(start + 2 * group * odd, group)] = other[...]


def applied(table, slots, row, blocks):
    vectors = jnp.concatenate([table[slots[s, row]] for s in range(blocks.shape[0])], axis=1)
    return lax.dot_general(vectors, lanes(blocks), LAST, preferred_element_type=jnp.float32)


def export_second_kernel(exports, slots, own, column, chip, other, degree, live, weights, out, table):
    fill_table(table, (own,), column, chip, other)
    for i in range(out.shape[0]):
        row = exports[i]
        product = applied(table, slots, row, weights[row])
        out[i] = (product / degree[pl.ds(row, 1), :] * live[pl.ds(row, 1), :]).astype(jnp.bfloat16)


def second_kernel(begin, slots, own, column, chip, other, degree, live, weights, passed, out, passed_out, table):
    fill_table(table, (own,), column, chip, other)
    passed_out[...] = passed[...]

    @pl.loop(0, out.shape[0] // ROWS_STEP)
    def _(step):
        for i in range(ROWS_STEP):
            place = step * ROWS_STEP + i
            row = begin + place
            product = applied(table, slots, row, weights[row])
            out[place] = (product / degree[pl.ds(row, 1), :] * live[pl.ds(row, 1), :]).astype(jnp.bfloat16)


def halves(value):
    high = value.astype(jnp.bfloat16)
    return high, (value - high.astype(jnp.float32)).astype(jnp.bfloat16)


def sketch_kernel(slots, low_own, high_own, column, chip, other, degree, live, weights, sketch, gram, table, sums):
    fill_table(table, (low_own, high_own), column, chip, other)
    row_blocks, _, size, _ = weights.shape
    columns = table.shape[1]
    sums[...] = jnp.zeros_like(sums)

    @pl.loop(0, row_blocks // ROWS_STEP)
    def _(step):
        highs, lows = [], []
        for i in range(ROWS_STEP):
            row = step * ROWS_STEP + i
            product = applied(table, slots, row, weights[row])
            value = product * lax.rsqrt(degree[pl.ds(row, 1), :]) * live[pl.ds(row, 1), :]
            sketch[:, pl.ds(pl.multiple_of(row * size, size), size)] = value
            high, low = halves(value)
            highs.append(high)
            lows.append(low)
        high = jnp.concatenate(highs, axis=1)
        both = jnp.concatenate([high, jnp.concatenate(lows, axis=1)], axis=0)
        sums[...] += lax.dot_general(both, high, LAST, preferred_element_type=jnp.float32)

    cross = sums[columns:]
    result = sums[:columns] + cross + cross.T
    gram[...] = jnp.concatenate([result[: columns // 2], result[columns // 2 :]], axis=1)


def factor_kernel(scale, grams, sketch, out, inverse):
    packed = grams[0]
    for i in range(1, grams.shape[0]):
        packed = packed + grams[i]
    half = packed.shape[0]
    count = 2 * half
    total = jnp.concatenate([packed[:, :count], packed[:, count:]], axis=0)
    identity = (
        lax.broadcasted_iota(jnp.int32, (count, count), 0) == lax.broadcasted_iota(jnp.int32, (count, count), 1)
    ).astype(jnp.float32)
    rest = jnp.concatenate([identity, total], axis=1)
    width = 8
    for start in range(0, count, width):
        height = rest.shape[0]
        sides = [
            jnp.broadcast_to(rest[:, count + start + j : count + start + j + 1], rest.shape) for j in range(width)
        ]
        below = lax.broadcasted_iota(jnp.int32, rest.shape, 0)
        for j in range(width):
            pivot = sides[j][j : j + 1, :]
            factors = jnp.where(below > j, sides[j] * (1.0 / pivot), 0.0)
            line = rest[j : j + 1, :]
            inverse[start + j : start + j + 1, :] = line * (lax.rsqrt(pivot) * scale)
            rest = rest - factors * line
            for k in range(j + 1, width):
                sides[k] = sides[k] - factors * sides[k][j : j + 1, :]
        if start + width < count:
            rest = rest[width:, :]
    high, low = halves(inverse[:, :count])
    value_high, value_low = halves(sketch[...])
    out[...] = (
        jnp.dot(high, value_high, preferred_element_type=jnp.float32)
        + jnp.dot(high, value_low, preferred_element_type=jnp.float32)
        + jnp.dot(low, value_high, preferred_element_type=jnp.float32)
    )


def cost(flops, moved):
    return pl.CostEstimate(flops=flops, bytes_accessed=moved, transcendentals=0)


SMEM = pl.BlockSpec(memory_space=pltpu.SMEM)
ANY = pl.BlockSpec(memory_space=pl.ANY)


def plain(kernel, in_specs, out_specs, out_shape, scratch, flops, moved):
    return pl.pallas_call(
        kernel,
        in_specs=in_specs,
        out_specs=out_specs,
        out_shape=out_shape,
        scratch_shapes=scratch,
        compiler_params=pltpu.CompilerParams(vmem_limit_bytes=LIMIT),
        cost_estimate=cost(flops, moved),
    )


def in_hbm(value):
    return pltpu.with_memory_space_constraint(value, pltpu.HBM)


class Kernels:
    def __init__(self, columns, row_blocks, slots, size, exports, halo):
        self.k, self.rb, self.nb, self.bs, self.eb = columns, row_blocks, slots, size, exports
        self.bytes_weights = row_blocks * slots * size * size * 2
        self.flops = 2 * columns * row_blocks * slots * size * size
        self.table = pltpu.VMEM((row_blocks + halo, columns, size), jnp.bfloat16)

    def export_first(self, exports, count, probe, weights):
        pieces = 4
        return plain(
            export_first_kernel,
            [SMEM, SMEM, ANY, ANY],
            VMEM,
            jax.ShapeDtypeStruct((self.eb, self.k, self.bs), jnp.bfloat16),
            [
                pltpu.VMEM((self.eb, self.k, self.bs), jnp.bfloat16),
                pltpu.VMEM((self.eb, self.nb, self.bs, self.bs), jnp.bfloat16),
                pltpu.SemaphoreType.DMA((self.eb,)),
                pltpu.SemaphoreType.DMA((self.eb, pieces)),
            ],
            self.flops // 16,
            self.bytes_weights // 16,
        )(exports, count, in_hbm(probe), in_hbm(weights))

    def first(self, count, probe, weights, passed):
        return plain(
            first_kernel,
            [SMEM, VMEM, VMEM, VMEM],
            [VMEM] * 4,
            [
                jax.ShapeDtypeStruct((self.rb, self.bs), jnp.float32),
                jax.ShapeDtypeStruct((self.rb, self.bs), jnp.float32),
                jax.ShapeDtypeStruct((self.rb, self.k, self.bs), jnp.bfloat16),
                jax.ShapeDtypeStruct(passed.shape, passed.dtype),
            ],
            [],
            self.flops,
            self.bytes_weights,
        )(count, probe, weights, passed)

    def export_second(self, exports, slots, tables, degree, live, weights):
        return plain(
            export_second_kernel,
            [SMEM] * 2 + [VMEM] * 7,
            VMEM,
            jax.ShapeDtypeStruct((self.eb, self.k, self.bs), jnp.bfloat16),
            [self.table],
            self.flops // 16,
            self.bytes_weights // 16,
        )(exports, slots, *tables, degree, live, weights)

    def second(self, begin, rows, slots, tables, degree, live, weights, passed):
        return plain(
            functools.partial(second_kernel, begin),
            [SMEM] + [VMEM] * 8,
            [VMEM, VMEM],
            [
                jax.ShapeDtypeStruct((rows, self.k, self.bs), jnp.bfloat16),
                jax.ShapeDtypeStruct(passed.shape, passed.dtype),
            ],
            [self.table],
            self.flops // 2,
            self.bytes_weights // 2,
        )(slots, *tables, degree, live, weights, passed)

    def sketch(self, slots, owns, halo, degree, live, weights):
        return plain(
            sketch_kernel,
            [SMEM] + [VMEM] * 8,
            [VMEM, VMEM],
            [
                jax.ShapeDtypeStruct((self.k, self.rb * self.bs), jnp.float32),
                jax.ShapeDtypeStruct((self.k // 2, 2 * self.k), jnp.float32),
            ],
            [self.table, pltpu.VMEM((2 * self.k, self.k), jnp.float32)],
            self.flops,
            self.bytes_weights,
        )(slots, *owns, *halo, degree, live, weights)

    def factor(self, scale, grams, sketch):
        return plain(
            functools.partial(factor_kernel, scale),
            [VMEM, VMEM],
            VMEM,
            jax.ShapeDtypeStruct(sketch.shape, jnp.float32),
            [pltpu.VMEM((self.k, 2 * self.k), jnp.float32)],
            6 * self.k * sketch.size,
            8 * sketch.size,
        )(grams, sketch)


def shifted(value, axis, step):
    count = lax.axis_size(axis)
    return lax.ppermute(value, axis, [(i, (i + step) % count) for i in range(count)])


def swapped(value, axis, partner):
    return lax.ppermute(value, axis, [(i, partner(i)) for i in range(lax.axis_size(axis))])


def along_narrow(exports):
    return shifted(exports, "narrow", 1), shifted(exports, "narrow", -1)


def halo_blocks(before, exports, after):
    count = lax.axis_size("wide")
    column = jnp.concatenate([before, exports, after], axis=0)
    chip = swapped(column, "wide", lambda i: i ^ 1)
    other = swapped(column, "wide", lambda i: (i + 1) % count if i % 2 else (i - 1) % count)
    return column, chip, other


def from_all(value, axis, groups=None):
    count = len(groups[0]) if groups else lax.axis_size(axis)
    copies = jnp.broadcast_to(value[None], (count, *value.shape))
    return lax.all_to_all(copies, axis, 0, 0, axis_index_groups=groups, tiled=True)


def gathered_grams(gram):
    chip = gram + swapped(gram, "wide", lambda i: i ^ 1)
    count = lax.axis_size("wide")
    groups = [list(range(core, count, 2)) for core in range(2)]
    return from_all(jnp.sum(from_all(chip, "wide", groups), axis=0), "narrow")


def local(test_matrix, weights, block_cols, export_rows, row_count):
    row_blocks, slots, size, _ = weights.shape
    columns, exports_each = test_matrix.shape[0], export_rows.shape[1]
    kernels = Kernels(columns, row_blocks, slots, size, exports_each, 9 * exports_each)
    part = lax.axis_index("wide") * lax.axis_size("narrow") + lax.axis_index("narrow")
    exports, slots_of = lax.dynamic_index_in_dim(export_rows, part, 0, keepdims=False), block_cols.T

    first_exports = kernels.export_first(exports, row_count, test_matrix, weights)
    before, after = along_narrow(first_exports)
    degree, live, first_input, passed = kernels.first(row_count, test_matrix, weights, first_exports)
    tables = (first_input, *halo_blocks(before, passed, after))
    second_exports = kernels.export_second(exports, slots_of, tables, degree, live, weights)
    before, after = along_narrow(second_exports)
    half = row_blocks // 2
    low, passed = kernels.second(0, half, slots_of, tables, degree, live, weights, second_exports)
    halo = halo_blocks(before, passed, after)
    high, _ = kernels.second(half, half, slots_of, tables, degree, live, weights, second_exports)
    sketch, gram = kernels.sketch(slots_of, (low, high), halo, degree, live, weights)
    grams = gathered_grams(gram)
    node_total = lax.axis_size(AXES) * row_blocks * size
    return kernels.factor(math.sqrt(node_total), grams, sketch)


def solution(mesh):
    in_specs = (
        P(None, AXES),
        P(AXES, None, None, None),
        P(AXES, None),
        P(),
        P(AXES),
    )
    return jax.shard_map(local, mesh=mesh, in_specs=in_specs, out_specs=P(None, AXES), check_vma=False)
```

```python
import functools
import math

import jax
import jax.numpy as jnp
from jax import lax
from jax.experimental import pallas as pl
from jax.experimental.pallas import tpu as pltpu
from jax.sharding import PartitionSpec as P

EPSILON = 1e-06
AXES = ("wide", "narrow")
ROWS_STEP = 8
VMEM = pl.BlockSpec(memory_space=pltpu.VMEM)
LIMIT = 24 * 1024 * 1024
LAST = (((1,), (1,)), ((), ()))


def lanes(blocks):
    return jnp.concatenate([blocks[i] for i in range(blocks.shape[0])], axis=1)


def block_degree(blocks):
    ones = jnp.ones((8, blocks.shape[0] * blocks.shape[2]), blocks.dtype)
    sums = lax.dot_general(lanes(jnp.abs(blocks)), ones, LAST, preferred_element_type=jnp.float32)
    return sums.T[0:1] + EPSILON


def live_mask(row, block_size, present):
    position = lax.broadcasted_iota(jnp.int32, (1, block_size), 1) + row * block_size
    return (position < present).astype(jnp.float32)


def scaled(probe, degree, live):
    return (probe.astype(jnp.float32) * lax.rsqrt(degree) * live).astype(jnp.bfloat16)


def export_first_kernel(
    exports, count, probe, weights, out, probe_here, weights_here, probe_sems, weights_sems
):
    pieces = weights_sems.shape[1]
    slots, size = weights.shape[1] // pieces, weights.shape[2]
    rows = [exports[i] for i in range(exports.shape[0])]
    copies = []
    for i, row in enumerate(rows):
        start = pl.multiple_of(row * size, size)
        copies.append(pltpu.make_async_copy(probe.at[:, pl.ds(start, size)], probe_here.at[i], probe_sems.at[i]))
        for j in range(pieces):
            some = pl.ds(j * slots, slots)
            copies.append(
                pltpu.make_async_copy(weights.at[row, some], weights_here.at[i, some], weights_sems.at[i, j])
            )
    for copy in copies:
        copy.start()
    for copy in copies:
        copy.wait()
    for i, row in enumerate(rows):
        live = live_mask(row, size, count[0])
        out[i] = scaled(probe_here[i], block_degree(weights_here[i]), live)


def first_kernel(count, probe, weights, degree_out, live_out, out):
    rows, size = weights.shape[0], weights.shape[2]

    @pl.loop(0, rows // ROWS_STEP)
    def _(step):
        for i in range(ROWS_STEP):
            row = step * ROWS_STEP + i
            degree = block_degree(weights[row])
            degree_out[pl.ds(row, 1), :] = degree
            live = live_mask(row, size, count[0])
            live_out[pl.ds(row, 1), :] = live
            out[row] = scaled(probe[:, pl.ds(pl.multiple_of(row * size, size), size)], degree, live)


def fill_table(table, owns, column, chip, other):
    start = 0
    for own in owns:
        table[start : start + own.shape[0]] = own[...]
        start += own.shape[0]
    group = column.shape[0]
    odd = lax.axis_index("wide") & 1
    table[start + group : start + 2 * group] = column[...]
    table[pl.ds(start + 2 * group * (1 - odd), group)] = chip[...]
    table[pl.ds(start + 2 * group * odd, group)] = other[...]


def applied(table, slots, row, blocks):
    vectors = jnp.concatenate([table[slots[s, row]] for s in range(blocks.shape[0])], axis=1)
    return lax.dot_general(lanes(blocks), vectors, LAST, preferred_element_type=jnp.float32).T


def export_second_kernel(exports, slots, own, column, chip, other, degree, live, weights, out, table):
    fill_table(table, (own,), column, chip, other)
    for i in range(out.shape[0]):
        row = exports[i]
        product = applied(table, slots, row, weights[row])
        out[i] = (product / degree[pl.ds(row, 1), :] * live[pl.ds(row, 1), :]).astype(jnp.bfloat16)


def second_kernel(begin, slots, own, column, chip, other, degree, live, weights, *rest):
    *passed, table = rest
    out = passed.pop(len(passed) // 2)
    if passed:
        passed[1][...] = passed[0][...]
    fill_table(table, (own,), column, chip, other)

    for place in range(out.shape[0]):
        row = begin + place
        product = applied(table, slots, row, weights[row])
        out[place] = (product / degree[row : row + 1, :] * live[row : row + 1, :]).astype(jnp.bfloat16)


def halves(value):
    high = value.astype(jnp.bfloat16)
    return high, (value - high.astype(jnp.float32)).astype(jnp.bfloat16)


def sketch_kernel(slots, low_own, high_own, column, chip, other, degree, live, weights, sketch, gram, table):
    fill_table(table, (low_own, high_own), column, chip, other)
    row_blocks, _, size, _ = weights.shape
    columns = table.shape[1]
    sums = jnp.zeros((2 * columns, columns), jnp.float32)
    for start in range(0, row_blocks, ROWS_STEP):
        for row in range(start, start + ROWS_STEP):
            product = applied(table, slots, row, weights[row])
            value = product * lax.rsqrt(degree[row : row + 1, :]) * live[row : row + 1, :]
            high, low = halves(value)
            sketch[:columns, row * size : (row + 1) * size] = high
            sketch[columns:, row * size : (row + 1) * size] = low
        some = slice(start * size, (start + ROWS_STEP) * size)
        sums = sums + lax.dot_general(
            sketch[:, some], sketch[:columns, some], LAST, preferred_element_type=jnp.float32
        )
    cross = sums[columns:]
    result = sums[:columns] + cross + cross.T
    gram[...] = jnp.concatenate([result[: columns // 2], result[columns // 2 :]], axis=1)


def factor_kernel(scale, grams, sketch, out, inverse, result, sems):
    packed = grams[0]
    for i in range(1, grams.shape[0]):
        packed = packed + grams[i]
    half = packed.shape[0]
    count = 2 * half
    total = jnp.concatenate([packed[:, :count], packed[:, count:]], axis=0)
    identity = (
        lax.broadcasted_iota(jnp.int32, (count, count), 0) == lax.broadcasted_iota(jnp.int32, (count, count), 1)
    ).astype(jnp.float32)
    rest = jnp.concatenate([identity, total], axis=1)
    width = 8
    for start in range(0, count, width):
        height = rest.shape[0]
        sides = [
            jnp.broadcast_to(rest[:, count + start + j : count + start + j + 1], rest.shape) for j in range(width)
        ]
        below = lax.broadcasted_iota(jnp.int32, rest.shape, 0)
        for j in range(width):
            pivot = sides[j][j : j + 1, :]
            factors = jnp.where(below > j, sides[j] * (1.0 / pivot), 0.0)
            line = rest[j : j + 1, :]
            inverse[start + j : start + j + 1, :] = line * (lax.rsqrt(pivot) * scale)
            rest = rest - factors * line
            for k in range(j + 1, width):
                sides[k] = sides[k] - factors * sides[k][j : j + 1, :]
        if start + width < count:
            rest = rest[width:, :]
    high, low = halves(inverse[:, :count])
    factors = jnp.concatenate(
        [jnp.concatenate([high, high], axis=1), jnp.concatenate([low, jnp.zeros_like(low)], axis=1)], axis=0
    )
    pieces = sems.shape[0]
    length = result.shape[1] // pieces
    copies = []
    for i in range(pieces):
        some = slice(i * length, (i + 1) * length)
        both = jnp.dot(factors, sketch[:, some], preferred_element_type=jnp.float32)
        result[:, some] = both[:count] + both[count:]
        copies.append(pltpu.make_async_copy(result.at[:, some], out.at[:, some], sems.at[i]))
        copies[i].start()
    for copy in copies:
        copy.wait()


def cost(flops, moved):
    return pl.CostEstimate(flops=flops, bytes_accessed=moved, transcendentals=0)


SMEM = pl.BlockSpec(memory_space=pltpu.SMEM)
ANY = pl.BlockSpec(memory_space=pl.ANY)


def plain(kernel, in_specs, out_specs, out_shape, scratch, flops, moved):
    return pl.pallas_call(
        kernel,
        in_specs=in_specs,
        out_specs=out_specs,
        out_shape=out_shape,
        scratch_shapes=scratch,
        compiler_params=pltpu.CompilerParams(vmem_limit_bytes=LIMIT),
        cost_estimate=cost(flops, moved),
    )


def in_hbm(value):
    return pltpu.with_memory_space_constraint(value, pltpu.HBM)


class Kernels:
    def __init__(self, columns, row_blocks, slots, size, exports, halo):
        self.k, self.rb, self.nb, self.bs, self.eb = columns, row_blocks, slots, size, exports
        self.bytes_weights = row_blocks * slots * size * size * 2
        self.flops = 2 * columns * row_blocks * slots * size * size
        self.table = pltpu.VMEM((row_blocks + halo, columns, size), jnp.bfloat16)

    def export_first(self, exports, count, probe, weights):
        pieces = 4
        return plain(
            export_first_kernel,
            [SMEM, SMEM, ANY, ANY],
            VMEM,
            jax.ShapeDtypeStruct((self.eb, self.k, self.bs), jnp.bfloat16),
            [
                pltpu.VMEM((self.eb, self.k, self.bs), jnp.bfloat16),
                pltpu.VMEM((self.eb, self.nb, self.bs, self.bs), jnp.bfloat16),
                pltpu.SemaphoreType.DMA((self.eb,)),
                pltpu.SemaphoreType.DMA((self.eb, pieces)),
            ],
            self.flops // 16,
            self.bytes_weights // 16,
        )(exports, count, in_hbm(probe), in_hbm(weights))

    def first(self, count, probe, weights):
        return plain(
            first_kernel,
            [SMEM, VMEM, VMEM],
            [VMEM] * 3,
            [
                jax.ShapeDtypeStruct((self.rb, self.bs), jnp.float32),
                jax.ShapeDtypeStruct((self.rb, self.bs), jnp.float32),
                jax.ShapeDtypeStruct((self.rb, self.k, self.bs), jnp.bfloat16),
            ],
            [],
            self.flops,
            self.bytes_weights,
        )(count, probe, weights)

    def export_second(self, exports, slots, tables, degree, live, weights):
        return plain(
            export_second_kernel,
            [SMEM] * 2 + [VMEM] * 7,
            VMEM,
            jax.ShapeDtypeStruct((self.eb, self.k, self.bs), jnp.bfloat16),
            [self.table],
            self.flops // 16,
            self.bytes_weights // 16,
        )(exports, slots, *tables, degree, live, weights)

    def second(self, begin, rows, slots, tables, degree, live, weights, *passed):
        shapes = [jax.ShapeDtypeStruct((rows, self.k, self.bs), jnp.bfloat16)]
        shapes += [jax.ShapeDtypeStruct(value.shape, value.dtype) for value in passed]
        return plain(
            functools.partial(second_kernel, begin),
            [SMEM] + [VMEM] * (7 + len(passed)),
            [VMEM] * len(shapes),
            shapes,
            [self.table],
            self.flops // 2,
            self.bytes_weights // 2,
        )(slots, *tables, degree, live, weights, *passed)

    def sketch(self, slots, owns, halo, degree, live, weights):
        return plain(
            sketch_kernel,
            [SMEM] + [VMEM] * 8,
            [VMEM, VMEM],
            [
                jax.ShapeDtypeStruct((2 * self.k, self.rb * self.bs), jnp.bfloat16),
                jax.ShapeDtypeStruct((self.k // 2, 2 * self.k), jnp.float32),
            ],
            [self.table],
            self.flops,
            self.bytes_weights,
        )(slots, *owns, *halo, degree, live, weights)

    def factor(self, scale, grams, sketch):
        shape = (self.k, sketch.shape[1])
        return plain(
            functools.partial(factor_kernel, scale),
            [VMEM, VMEM],
            ANY,
            jax.ShapeDtypeStruct(shape, jnp.float32),
            [
                pltpu.VMEM((self.k, 2 * self.k), jnp.float32),
                pltpu.VMEM(shape, jnp.float32),
                pltpu.SemaphoreType.DMA((4,)),
            ],
            6 * self.k * sketch.size,
            4 * sketch.size,
        )(grams, sketch)


def shifted(value, axis, step):
    count = lax.axis_size(axis)
    return lax.ppermute(value, axis, [(i, (i + step) % count) for i in range(count)])


def swapped(value, axis, partner):
    return lax.ppermute(value, axis, [(i, partner(i)) for i in range(lax.axis_size(axis))])


def along_narrow(exports):
    return shifted(exports, "narrow", 1), shifted(exports, "narrow", -1)


def halo_blocks(before, exports, after):
    count = lax.axis_size("wide")
    column = jnp.concatenate([before, exports, after], axis=0)
    other = swapped(column, "wide", lambda i: (i + 1) % count if i % 2 else (i - 1) % count)
    chip = swapped(column, "wide", lambda i: i ^ 1)
    return column, chip, other


def from_all(value, axis, groups=None):
    count = len(groups[0]) if groups else lax.axis_size(axis)
    copies = jnp.broadcast_to(value[None], (count, *value.shape))
    return lax.all_to_all(copies, axis, 0, 0, axis_index_groups=groups, tiled=True)


def gathered_grams(gram):
    chip = gram + swapped(gram, "wide", lambda i: i ^ 1)
    count = lax.axis_size("wide")
    groups = [list(range(core, count, 2)) for core in range(2)]
    return from_all(jnp.sum(from_all(chip, "wide", groups), axis=0), "narrow")


def local(test_matrix, weights, block_cols, export_rows, row_count):
    row_blocks, slots, size, _ = weights.shape
    columns, exports_each = test_matrix.shape[0], export_rows.shape[1]
    kernels = Kernels(columns, row_blocks, slots, size, exports_each, 9 * exports_each)
    part = lax.axis_index("wide") * lax.axis_size("narrow") + lax.axis_index("narrow")
    exports, slots_of = lax.dynamic_index_in_dim(export_rows, part, 0, keepdims=False), block_cols.T

    first_exports = kernels.export_first(exports, row_count, test_matrix, weights)
    before, after = along_narrow(first_exports)
    degree, live, first_input = kernels.first(row_count, test_matrix, weights)
    tables = (first_input, *halo_blocks(before, first_exports, after))
    second_exports = kernels.export_second(exports, slots_of, tables, degree, live, weights)
    before, after = along_narrow(second_exports)
    half = row_blocks // 2
    low, passed = kernels.second(0, half, slots_of, tables, degree, live, weights, second_exports)
    halo = halo_blocks(before, passed, after)
    (high,) = kernels.second(half, half, slots_of, tables, degree, live, weights)
    sketch, gram = kernels.sketch(slots_of, (low, high), halo, degree, live, weights)
    grams = gathered_grams(gram)
    node_total = lax.axis_size(AXES) * row_blocks * size
    return kernels.factor(math.sqrt(node_total), grams, sketch)


def solution(mesh):
    in_specs = (
        P(None, AXES),
        P(AXES, None, None, None),
        P(AXES, None),
        P(),
        P(AXES),
    )
    return jax.shard_map(local, mesh=mesh, in_specs=in_specs, out_specs=P(None, AXES), check_vma=False)
```

```python
import functools
import math

import jax
import jax.numpy as jnp
from jax import lax
from jax.experimental import pallas as pl
from jax.experimental.pallas import tpu as pltpu
from jax.sharding import PartitionSpec as P

EPSILON = 1e-06
AXES = ("wide", "narrow")
ROWS_STEP = 8
VMEM = pl.BlockSpec(memory_space=pltpu.VMEM)
LIMIT = 24 * 1024 * 1024
LAST = (((1,), (1,)), ((), ()))


def lanes(blocks):
    return jnp.concatenate([blocks[i] for i in range(blocks.shape[0])], axis=1)


def block_degree(blocks):
    ones = jnp.ones((8, blocks.shape[0] * blocks.shape[2]), blocks.dtype)
    sums = lax.dot_general(lanes(jnp.abs(blocks)), ones, LAST, preferred_element_type=jnp.float32)
    return sums.T[0:1] + EPSILON


def live_mask(row, block_size, present):
    position = lax.broadcasted_iota(jnp.int32, (1, block_size), 1) + row * block_size
    return (position < present).astype(jnp.float32)


def scaled(probe, degree, live):
    return (probe.astype(jnp.float32) * lax.rsqrt(degree) * live).astype(jnp.bfloat16)


def export_first_kernel(
    exports, count, probe, weights, out, probe_here, weights_here, probe_sems, weights_sems
):
    pieces = weights_sems.shape[1]
    slots, size = weights.shape[1] // pieces, weights.shape[2]
    rows = [exports[i] for i in range(exports.shape[0])]
    copies = []
    for i, row in enumerate(rows):
        start = pl.multiple_of(row * size, size)
        copies.append(pltpu.make_async_copy(probe.at[:, pl.ds(start, size)], probe_here.at[i], probe_sems.at[i]))
        for j in range(pieces):
            some = pl.ds(j * slots, slots)
            copies.append(
                pltpu.make_async_copy(weights.at[row, some], weights_here.at[i, some], weights_sems.at[i, j])
            )
    for copy in copies:
        copy.start()
    for copy in copies:
        copy.wait()
    for i, row in enumerate(rows):
        live = live_mask(row, size, count[0])
        out[i] = scaled(probe_here[i], block_degree(weights_here[i]), live)


def first_kernel(count, probe, weights, degree_out, live_out, out):
    rows, size = weights.shape[0], weights.shape[2]

    @pl.loop(0, rows // ROWS_STEP)
    def _(step):
        for i in range(ROWS_STEP):
            row = step * ROWS_STEP + i
            degree = block_degree(weights[row])
            degree_out[pl.ds(row, 1), :] = degree
            live = live_mask(row, size, count[0])
            live_out[pl.ds(row, 1), :] = live
            out[row] = scaled(probe[:, pl.ds(pl.multiple_of(row * size, size), size)], degree, live)


def fill_table(table, owns, column, chip, other):
    start = 0
    for own in owns:
        table[start : start + own.shape[0]] = own[...]
        start += own.shape[0]
    group = column.shape[0]
    odd = lax.axis_index("wide") & 1
    table[start + group : start + 2 * group] = column[...]
    table[pl.ds(start + 2 * group * (1 - odd), group)] = chip[...]
    table[pl.ds(start + 2 * group * odd, group)] = other[...]


def applied(table, slots, row, blocks):
    vectors = jnp.concatenate([table[slots[s, row]] for s in range(blocks.shape[0])], axis=1)
    return lax.dot_general(lanes(blocks), vectors, LAST, preferred_element_type=jnp.float32).T


def export_second_kernel(exports, slots, own, column, chip, other, degree, live, weights, out, table):
    fill_table(table, (own,), column, chip, other)
    for i in range(out.shape[0]):
        row = exports[i]
        product = applied(table, slots, row, weights[row])
        out[i] = (product / degree[pl.ds(row, 1), :] * live[pl.ds(row, 1), :]).astype(jnp.bfloat16)


def second_kernel(begin, slots, own, column, chip, other, degree, live, weights, *rest):
    *passed, table = rest
    out = passed.pop(len(passed) // 2)
    if passed:
        passed[1][...] = passed[0][...]
    fill_table(table, (own,), column, chip, other)

    for place in range(out.shape[0]):
        row = begin + place
        product = applied(table, slots, row, weights[row])
        out[place] = (product / degree[row : row + 1, :] * live[row : row + 1, :]).astype(jnp.bfloat16)


def halves(value):
    high = value.astype(jnp.bfloat16)
    return high, (value - high.astype(jnp.float32)).astype(jnp.bfloat16)


def grid(size):
    shape = (size, size)
    return lax.broadcasted_iota(jnp.int32, shape, 0), lax.broadcasted_iota(jnp.int32, shape, 1)


def packed(square):
    half = square.shape[0] // 2
    down, along = grid(half)
    first, mixed, last = square[:half, :half], square[half:, :half], square[half:, half:]
    both = jnp.concatenate([mixed, jnp.where(down >= along, first, last)], axis=1)
    lines = jnp.concatenate([both[: half // 2], both[half // 2 :]], axis=1)
    diagonal = jnp.sum(jnp.where(down == along, last, 0.0), axis=0, keepdims=True)
    diagonal = jnp.concatenate([diagonal] * (lines.shape[1] // half), axis=1)
    return [lines[i : i + 1] for i in range(half // 2)] + [diagonal]


def unpacked(lines, diagonal):
    half = 2 * lines.shape[0]
    down, along = grid(half)
    both = jnp.concatenate([lines[:, : 2 * half], lines[:, 2 * half :]], axis=0)
    mixed, triangles = both[:, :half], both[:, half:]
    turned = triangles.T
    first = jnp.where(down >= along, triangles, turned)
    last = jnp.where(down < along, triangles, jnp.where(down > along, turned, diagonal[:, :half]))
    return jnp.concatenate(
        [jnp.concatenate([first, mixed.T], axis=1), jnp.concatenate([mixed, last], axis=1)], axis=0
    )


def sketch_kernel(slots, low_own, high_own, column, chip, other, degree, live, weights, sketch, gram, table):
    fill_table(table, (low_own, high_own), column, chip, other)
    row_blocks, _, size, _ = weights.shape
    columns = table.shape[1]
    sums = jnp.zeros((2 * columns, columns), jnp.float32)
    for start in range(0, row_blocks, ROWS_STEP):
        for row in range(start, start + ROWS_STEP):
            product = applied(table, slots, row, weights[row])
            value = product * lax.rsqrt(degree[row : row + 1, :]) * live[row : row + 1, :]
            high, low = halves(value)
            sketch[:columns, row * size : (row + 1) * size] = high
            sketch[columns:, row * size : (row + 1) * size] = low
        some = slice(start * size, (start + ROWS_STEP) * size)
        sums = sums + lax.dot_general(
            sketch[:, some], sketch[:columns, some], LAST, preferred_element_type=jnp.float32
        )
    cross = sums[columns:]
    result = sums[:columns] + cross + cross.T
    for i, line in enumerate(packed(result)):
        gram[:, i * size : (i + 1) * size] = line


def factor_kernel(scale, grams, sketch, out, inverse, result, lines, sems):
    sums = grams[0]
    for i in range(1, grams.shape[0]):
        sums = sums + grams[i]
    size = lines.shape[1]
    for i in range(lines.shape[0]):
        lines[i : i + 1, :] = sums[:, i * size : (i + 1) * size]
    last = lines.shape[0] - 1
    total = unpacked(lines[:last], lines[last:])
    count = total.shape[0]
    down, along = grid(count)
    rest = jnp.concatenate([(down == along).astype(jnp.float32), total], axis=1)
    width = 16
    for start in range(0, count, width):
        sides = [
            jnp.broadcast_to(rest[:, count + start + j : count + start + j + 1], rest.shape) for j in range(width)
        ]
        below = lax.broadcasted_iota(jnp.int32, rest.shape, 0)
        for j in range(width):
            pivot = sides[j][j : j + 1, :]
            factors = jnp.where(below > j, sides[j] * (1.0 / pivot), 0.0)
            line = rest[j : j + 1, :]
            inverse[start + j : start + j + 1, :] = line * (lax.rsqrt(pivot) * scale)
            rest = rest - factors * line
            for k in range(j + 1, width):
                sides[k] = sides[k] - factors * sides[k][j : j + 1, :]
        if start + width < count:
            rest = rest[width:, :]
    high, low = halves(inverse[:, :count])
    factors = jnp.concatenate(
        [jnp.concatenate([high, high], axis=1), jnp.concatenate([low, jnp.zeros_like(low)], axis=1)], axis=0
    )
    pieces = sems.shape[0]
    length = result.shape[1] // pieces
    copies = []
    for i in range(pieces):
        some = slice(i * length, (i + 1) * length)
        both = jnp.dot(factors, sketch[:, some], preferred_element_type=jnp.float32)
        result[:, some] = both[:count] + both[count:]
        copies.append(pltpu.make_async_copy(result.at[:, some], out.at[:, some], sems.at[i]))
        copies[i].start()
    for copy in copies:
        copy.wait()


def cost(flops, moved):
    return pl.CostEstimate(flops=flops, bytes_accessed=moved, transcendentals=0)


SMEM = pl.BlockSpec(memory_space=pltpu.SMEM)
ANY = pl.BlockSpec(memory_space=pl.ANY)


def plain(kernel, in_specs, out_specs, out_shape, scratch, flops, moved):
    return pl.pallas_call(
        kernel,
        in_specs=in_specs,
        out_specs=out_specs,
        out_shape=out_shape,
        scratch_shapes=scratch,
        compiler_params=pltpu.CompilerParams(vmem_limit_bytes=LIMIT),
        cost_estimate=cost(flops, moved),
    )


def in_hbm(value):
    return pltpu.with_memory_space_constraint(value, pltpu.HBM)


class Kernels:
    def __init__(self, columns, row_blocks, slots, size, exports, halo):
        self.k, self.rb, self.nb, self.bs, self.eb = columns, row_blocks, slots, size, exports
        self.bytes_weights = row_blocks * slots * size * size * 2
        self.flops = 2 * columns * row_blocks * slots * size * size
        self.table = pltpu.VMEM((row_blocks + halo, columns, size), jnp.bfloat16)

    def export_first(self, exports, count, probe, weights):
        pieces = 4
        return plain(
            export_first_kernel,
            [SMEM, SMEM, ANY, ANY],
            VMEM,
            jax.ShapeDtypeStruct((self.eb, self.k, self.bs), jnp.bfloat16),
            [
                pltpu.VMEM((self.eb, self.k, self.bs), jnp.bfloat16),
                pltpu.VMEM((self.eb, self.nb, self.bs, self.bs), jnp.bfloat16),
                pltpu.SemaphoreType.DMA((self.eb,)),
                pltpu.SemaphoreType.DMA((self.eb, pieces)),
            ],
            self.flops // 16,
            self.bytes_weights // 16,
        )(exports, count, in_hbm(probe), in_hbm(weights))

    def first(self, count, probe, weights):
        return plain(
            first_kernel,
            [SMEM, VMEM, VMEM],
            [VMEM] * 3,
            [
                jax.ShapeDtypeStruct((self.rb, self.bs), jnp.float32),
                jax.ShapeDtypeStruct((self.rb, self.bs), jnp.float32),
                jax.ShapeDtypeStruct((self.rb, self.k, self.bs), jnp.bfloat16),
            ],
            [],
            self.flops,
            self.bytes_weights,
        )(count, probe, weights)

    def export_second(self, exports, slots, tables, degree, live, weights):
        return plain(
            export_second_kernel,
            [SMEM] * 2 + [VMEM] * 7,
            VMEM,
            jax.ShapeDtypeStruct((self.eb, self.k, self.bs), jnp.bfloat16),
            [self.table],
            self.flops // 16,
            self.bytes_weights // 16,
        )(exports, slots, *tables, degree, live, weights)

    def second(self, begin, rows, slots, tables, degree, live, weights, *passed):
        shapes = [jax.ShapeDtypeStruct((rows, self.k, self.bs), jnp.bfloat16)]
        shapes += [jax.ShapeDtypeStruct(value.shape, value.dtype) for value in passed]
        return plain(
            functools.partial(second_kernel, begin),
            [SMEM] + [VMEM] * (7 + len(passed)),
            [VMEM] * len(shapes),
            shapes,
            [self.table],
            self.flops // 2,
            self.bytes_weights // 2,
        )(slots, *tables, degree, live, weights, *passed)

    def sketch(self, slots, owns, halo, degree, live, weights):
        return plain(
            sketch_kernel,
            [SMEM] + [VMEM] * 8,
            [VMEM, VMEM],
            [
                jax.ShapeDtypeStruct((2 * self.k, self.rb * self.bs), jnp.bfloat16),
                jax.ShapeDtypeStruct((1, (self.k // 4 + 1) * self.bs), jnp.float32),
            ],
            [self.table],
            self.flops,
            self.bytes_weights,
        )(slots, *owns, *halo, degree, live, weights)

    def factor(self, scale, grams, sketch):
        shape = (self.k, sketch.shape[1])
        return plain(
            functools.partial(factor_kernel, scale),
            [VMEM, VMEM],
            ANY,
            jax.ShapeDtypeStruct(shape, jnp.float32),
            [
                pltpu.VMEM((self.k, 2 * self.k), jnp.float32),
                pltpu.VMEM(shape, jnp.float32),
                pltpu.VMEM((self.k // 4 + 1, self.bs), jnp.float32),
                pltpu.SemaphoreType.DMA((4,)),
            ],
            6 * self.k * sketch.size,
            4 * sketch.size,
        )(grams, sketch)


def shifted(value, axis, step):
    count = lax.axis_size(axis)
    return lax.ppermute(value, axis, [(i, (i + step) % count) for i in range(count)])


def swapped(value, axis, partner):
    return lax.ppermute(value, axis, [(i, partner(i)) for i in range(lax.axis_size(axis))])


def along_narrow(exports):
    return shifted(exports, "narrow", 1), shifted(exports, "narrow", -1)


def halo_blocks(before, exports, after):
    count = lax.axis_size("wide")
    column = jnp.concatenate([before, exports, after], axis=0)
    other = swapped(column, "wide", lambda i: (i + 1) % count if i % 2 else (i - 1) % count)
    chip = swapped(column, "wide", lambda i: i ^ 1)
    return column, chip, other


def from_all(value, axis, groups=None):
    count = len(groups[0]) if groups else lax.axis_size(axis)
    copies = jnp.broadcast_to(value[None], (count, *value.shape))
    return lax.all_to_all(copies, axis, 0, 0, axis_index_groups=groups, tiled=True)


def gathered_grams(gram):
    chip = gram + swapped(gram, "wide", lambda i: i ^ 1)
    count = lax.axis_size("wide")
    groups = [list(range(core, count, 2)) for core in range(2)]
    return from_all(jnp.sum(from_all(chip, "wide", groups), axis=0), "narrow")


def local(test_matrix, weights, block_cols, export_rows, row_count):
    row_blocks, slots, size, _ = weights.shape
    columns, exports_each = test_matrix.shape[0], export_rows.shape[1]
    kernels = Kernels(columns, row_blocks, slots, size, exports_each, 9 * exports_each)
    part = lax.axis_index("wide") * lax.axis_size("narrow") + lax.axis_index("narrow")
    exports, slots_of = lax.dynamic_index_in_dim(export_rows, part, 0, keepdims=False), block_cols.T

    first_exports = kernels.export_first(exports, row_count, test_matrix, weights)
    before, after = along_narrow(first_exports)
    degree, live, first_input = kernels.first(row_count, test_matrix, weights)
    tables = (first_input, *halo_blocks(before, first_exports, after))
    second_exports = kernels.export_second(exports, slots_of, tables, degree, live, weights)
    before, after = along_narrow(second_exports)
    half = row_blocks // 2
    low, passed = kernels.second(0, half, slots_of, tables, degree, live, weights, second_exports)
    halo = halo_blocks(before, passed, after)
    (high,) = kernels.second(half, half, slots_of, tables, degree, live, weights)
    sketch, gram = kernels.sketch(slots_of, (low, high), halo, degree, live, weights)
    grams = gathered_grams(gram)
    node_total = lax.axis_size(AXES) * row_blocks * size
    return kernels.factor(math.sqrt(node_total), grams, sketch)


def solution(mesh):
    in_specs = (
        P(None, AXES),
        P(AXES, None, None, None),
        P(AXES, None),
        P(),
        P(AXES),
    )
    return jax.shard_map(local, mesh=mesh, in_specs=in_specs, out_specs=P(None, AXES), check_vma=False)
```

```python
import functools
import math

import jax
import jax.numpy as jnp
from jax import lax
from jax.experimental import pallas as pl
from jax.experimental.pallas import tpu as pltpu
from jax.sharding import PartitionSpec as P

EPSILON = 1e-06
AXES = ("wide", "narrow")
ROWS_STEP = 8
VMEM = pl.BlockSpec(memory_space=pltpu.VMEM)
LIMIT = 24 * 1024 * 1024
LAST = (((1,), (1,)), ((), ()))


def lanes(blocks):
    return jnp.concatenate([blocks[i] for i in range(blocks.shape[0])], axis=1)


def block_degree(blocks):
    ones = jnp.ones((8, blocks.shape[0] * blocks.shape[2]), blocks.dtype)
    sums = lax.dot_general(lanes(jnp.abs(blocks)), ones, LAST, preferred_element_type=jnp.float32)
    return sums.T[0:1] + EPSILON


def live_mask(row, block_size, present):
    position = lax.broadcasted_iota(jnp.int32, (1, block_size), 1) + row * block_size
    return (position < present).astype(jnp.float32)


def scaled(probe, degree, live):
    return (probe.astype(jnp.float32) * lax.rsqrt(degree) * live).astype(jnp.bfloat16)


def export_first_kernel(
    exports, count, probe, weights, out, probe_here, weights_here, probe_sems, weights_sems
):
    pieces = weights_sems.shape[1]
    slots, size = weights.shape[1] // pieces, weights.shape[2]
    rows = [exports[i] for i in range(exports.shape[0])]
    copies = []
    for i, row in enumerate(rows):
        start = pl.multiple_of(row * size, size)
        copies.append(pltpu.make_async_copy(probe.at[:, pl.ds(start, size)], probe_here.at[i], probe_sems.at[i]))
        for j in range(pieces):
            some = pl.ds(j * slots, slots)
            copies.append(
                pltpu.make_async_copy(weights.at[row, some], weights_here.at[i, some], weights_sems.at[i, j])
            )
    for copy in copies:
        copy.start()
    for copy in copies:
        copy.wait()
    for i, row in enumerate(rows):
        live = live_mask(row, size, count[0])
        out[i] = scaled(probe_here[i], block_degree(weights_here[i]), live)


def first_kernel(count, probe, weights, degree_out, live_out, out):
    rows, size = weights.shape[0], weights.shape[2]

    @pl.loop(0, rows // ROWS_STEP)
    def _(step):
        for i in range(ROWS_STEP):
            row = step * ROWS_STEP + i
            degree = block_degree(weights[row])
            degree_out[pl.ds(row, 1), :] = degree
            live = live_mask(row, size, count[0])
            live_out[pl.ds(row, 1), :] = live
            out[row] = scaled(probe[:, pl.ds(pl.multiple_of(row * size, size), size)], degree, live)


def fill_table(table, own, column, chip, other):
    start = own.shape[0]
    table[:start] = own[...]
    group = column.shape[0]
    odd = lax.axis_index("wide") & 1
    table[start + group : start + 2 * group] = column[...]
    table[pl.ds(start + 2 * group * (1 - odd), group)] = chip[...]
    table[pl.ds(start + 2 * group * odd, group)] = other[...]


def applied(table, slots, row, blocks):
    vectors = jnp.concatenate([table[slots[s, row]] for s in range(blocks.shape[0])], axis=1)
    return lax.dot_general(lanes(blocks), vectors, LAST, preferred_element_type=jnp.float32).T


def export_second_kernel(exports, slots, own, column, chip, other, degree, live, weights, out, table):
    fill_table(table, own, column, chip, other)
    for i in range(out.shape[0]):
        row = exports[i]
        product = applied(table, slots, row, weights[row])
        out[i] = (product / degree[pl.ds(row, 1), :] * live[pl.ds(row, 1), :]).astype(jnp.bfloat16)


def second_kernel(slots, own, column, chip, other, degree, live, weights, out, table):
    fill_table(table, own, column, chip, other)
    for row in range(out.shape[0]):
        product = applied(table, slots, row, weights[row])
        out[row] = (product / degree[row : row + 1, :] * live[row : row + 1, :]).astype(jnp.bfloat16)


def halves(value):
    high = value.astype(jnp.bfloat16)
    return high, (value - high.astype(jnp.float32)).astype(jnp.bfloat16)


def grid(size):
    shape = (size, size)
    return lax.broadcasted_iota(jnp.int32, shape, 0), lax.broadcasted_iota(jnp.int32, shape, 1)


def packed(square):
    half = square.shape[0] // 2
    down, along = grid(half)
    first, mixed, last = square[:half, :half], square[half:, :half], square[half:, half:]
    both = jnp.concatenate([mixed, jnp.where(down >= along, first, last)], axis=1)
    lines = jnp.concatenate([both[: half // 2], both[half // 2 :]], axis=1)
    diagonal = jnp.sum(jnp.where(down == along, last, 0.0), axis=0, keepdims=True)
    diagonal = jnp.concatenate([diagonal] * (lines.shape[1] // half), axis=1)
    return [lines[i : i + 1] for i in range(half // 2)] + [diagonal]


def unpacked(lines, diagonal):
    half = 2 * lines.shape[0]
    down, along = grid(half)
    both = jnp.concatenate([lines[:, : 2 * half], lines[:, 2 * half :]], axis=0)
    mixed, triangles = both[:, :half], both[:, half:]
    turned = triangles.T
    first = jnp.where(down >= along, triangles, turned)
    last = jnp.where(down < along, triangles, jnp.where(down > along, turned, diagonal[:, :half]))
    return jnp.concatenate(
        [jnp.concatenate([first, mixed.T], axis=1), jnp.concatenate([mixed, last], axis=1)], axis=0
    )


def sketch_kernel(slots, own, column, chip, other, degree, live, weights, sketch, gram, table):
    fill_table(table, own, column, chip, other)
    row_blocks, _, size, _ = weights.shape
    columns = table.shape[1]
    sums = jnp.zeros((2 * columns, columns), jnp.float32)
    for start in range(0, row_blocks, ROWS_STEP):
        for row in range(start, start + ROWS_STEP):
            product = applied(table, slots, row, weights[row])
            value = product * lax.rsqrt(degree[row : row + 1, :]) * live[row : row + 1, :]
            high, low = halves(value)
            sketch[:columns, row * size : (row + 1) * size] = high
            sketch[columns:, row * size : (row + 1) * size] = low
        some = slice(start * size, (start + ROWS_STEP) * size)
        sums = sums + lax.dot_general(
            sketch[:, some], sketch[:columns, some], LAST, preferred_element_type=jnp.float32
        )
    cross = sums[columns:]
    result = sums[:columns] + cross + cross.T
    for i, line in enumerate(packed(result)):
        gram[:, i * size : (i + 1) * size] = line


def factor_kernel(scale, grams, sketch, out, inverse, result, lines, sems):
    sums = grams[0]
    for i in range(1, grams.shape[0]):
        sums = sums + grams[i]
    size = lines.shape[1]
    for i in range(lines.shape[0]):
        lines[i : i + 1, :] = sums[:, i * size : (i + 1) * size]
    last = lines.shape[0] - 1
    total = unpacked(lines[:last], lines[last:])
    count = total.shape[0]
    down, along = grid(count)
    rest = jnp.concatenate([(down == along).astype(jnp.float32), total], axis=1)
    width = 16
    for start in range(0, count, width):
        sides = [
            jnp.broadcast_to(rest[:, count + start + j : count + start + j + 1], rest.shape) for j in range(width)
        ]
        below = lax.broadcasted_iota(jnp.int32, rest.shape, 0)
        for j in range(width):
            pivot = sides[j][j : j + 1, :]
            factors = jnp.where(below > j, sides[j] * (1.0 / pivot), 0.0)
            line = rest[j : j + 1, :]
            inverse[start + j : start + j + 1, :] = line * (lax.rsqrt(pivot) * scale)
            rest = rest - factors * line
            for k in range(j + 1, width):
                sides[k] = sides[k] - factors * sides[k][j : j + 1, :]
        if start + width < count:
            rest = rest[width:, :]
    high, low = halves(inverse[:, :count])
    factors = jnp.concatenate(
        [jnp.concatenate([high, high], axis=1), jnp.concatenate([low, jnp.zeros_like(low)], axis=1)], axis=0
    )
    pieces = sems.shape[0]
    length = result.shape[1] // pieces
    copies = []
    for i in range(pieces):
        some = slice(i * length, (i + 1) * length)
        both = jnp.dot(factors, sketch[:, some], preferred_element_type=jnp.float32)
        result[:, some] = both[:count] + both[count:]
        copies.append(pltpu.make_async_copy(result.at[:, some], out.at[:, some], sems.at[i]))
        copies[i].start()
    for copy in copies:
        copy.wait()


def cost(flops, moved):
    return pl.CostEstimate(flops=flops, bytes_accessed=moved, transcendentals=0)


SMEM = pl.BlockSpec(memory_space=pltpu.SMEM)
ANY = pl.BlockSpec(memory_space=pl.ANY)


def plain(kernel, in_specs, out_specs, out_shape, scratch, flops, moved):
    return pl.pallas_call(
        kernel,
        in_specs=in_specs,
        out_specs=out_specs,
        out_shape=out_shape,
        scratch_shapes=scratch,
        compiler_params=pltpu.CompilerParams(vmem_limit_bytes=LIMIT),
        cost_estimate=cost(flops, moved),
    )


def in_hbm(value):
    return pltpu.with_memory_space_constraint(value, pltpu.HBM)


class Kernels:
    def __init__(self, columns, row_blocks, slots, size, exports, halo):
        self.k, self.rb, self.nb, self.bs, self.eb = columns, row_blocks, slots, size, exports
        self.bytes_weights = row_blocks * slots * size * size * 2
        self.flops = 2 * columns * row_blocks * slots * size * size
        self.table = pltpu.VMEM((row_blocks + halo, columns, size), jnp.bfloat16)

    def export_first(self, exports, count, probe, weights):
        pieces = 4
        return plain(
            export_first_kernel,
            [SMEM, SMEM, ANY, ANY],
            VMEM,
            jax.ShapeDtypeStruct((self.eb, self.k, self.bs), jnp.bfloat16),
            [
                pltpu.VMEM((self.eb, self.k, self.bs), jnp.bfloat16),
                pltpu.VMEM((self.eb, self.nb, self.bs, self.bs), jnp.bfloat16),
                pltpu.SemaphoreType.DMA((self.eb,)),
                pltpu.SemaphoreType.DMA((self.eb, pieces)),
            ],
            self.flops // 16,
            self.bytes_weights // 16,
        )(exports, count, in_hbm(probe), in_hbm(weights))

    def first(self, count, probe, weights):
        return plain(
            first_kernel,
            [SMEM, VMEM, VMEM],
            [VMEM] * 3,
            [
                jax.ShapeDtypeStruct((self.rb, self.bs), jnp.float32),
                jax.ShapeDtypeStruct((self.rb, self.bs), jnp.float32),
                jax.ShapeDtypeStruct((self.rb, self.k, self.bs), jnp.bfloat16),
            ],
            [],
            self.flops,
            self.bytes_weights,
        )(count, probe, weights)

    def export_second(self, exports, slots, tables, degree, live, weights):
        return plain(
            export_second_kernel,
            [SMEM] * 2 + [VMEM] * 7,
            VMEM,
            jax.ShapeDtypeStruct((self.eb, self.k, self.bs), jnp.bfloat16),
            [self.table],
            self.flops // 16,
            self.bytes_weights // 16,
        )(exports, slots, *tables, degree, live, weights)

    def second(self, slots, tables, degree, live, weights):
        return plain(
            second_kernel,
            [SMEM] + [VMEM] * 7,
            VMEM,
            jax.ShapeDtypeStruct((self.rb, self.k, self.bs), jnp.bfloat16),
            [self.table],
            self.flops,
            self.bytes_weights,
        )(slots, *tables, degree, live, weights)

    def sketch(self, slots, own, halo, degree, live, weights):
        return plain(
            sketch_kernel,
            [SMEM] + [VMEM] * 7,
            [VMEM, VMEM],
            [
                jax.ShapeDtypeStruct((2 * self.k, self.rb * self.bs), jnp.bfloat16),
                jax.ShapeDtypeStruct((1, (self.k // 4 + 1) * self.bs), jnp.float32),
            ],
            [self.table],
            self.flops,
            self.bytes_weights,
        )(slots, own, *halo, degree, live, weights)

    def factor(self, scale, grams, sketch):
        shape = (self.k, sketch.shape[1])
        return plain(
            functools.partial(factor_kernel, scale),
            [VMEM, VMEM],
            ANY,
            jax.ShapeDtypeStruct(shape, jnp.float32),
            [
                pltpu.VMEM((self.k, 2 * self.k), jnp.float32),
                pltpu.VMEM(shape, jnp.float32),
                pltpu.VMEM((self.k // 4 + 1, self.bs), jnp.float32),
                pltpu.SemaphoreType.DMA((8,)),
            ],
            6 * self.k * sketch.size,
            4 * sketch.size,
        )(grams, sketch)


def shifted(value, axis, step):
    count = lax.axis_size(axis)
    return lax.ppermute(value, axis, [(i, (i + step) % count) for i in range(count)])


def swapped(value, axis, partner):
    return lax.ppermute(value, axis, [(i, partner(i)) for i in range(lax.axis_size(axis))])


def along_narrow(exports):
    return shifted(exports, "narrow", 1), shifted(exports, "narrow", -1)


def halo_blocks(before, exports, after):
    count = lax.axis_size("wide")
    column = jnp.concatenate([before, exports, after], axis=0)
    other = swapped(column, "wide", lambda i: (i + 1) % count if i % 2 else (i - 1) % count)
    chip = swapped(column, "wide", lambda i: i ^ 1)
    return column, chip, other


def from_all(value, axis, groups=None):
    count = len(groups[0]) if groups else lax.axis_size(axis)
    copies = jnp.broadcast_to(value[None], (count, *value.shape))
    return lax.all_to_all(copies, axis, 0, 0, axis_index_groups=groups, tiled=True)


def gathered_grams(gram):
    chip = gram + swapped(gram, "wide", lambda i: i ^ 1)
    count = lax.axis_size("wide")
    groups = [list(range(core, count, 2)) for core in range(2)]
    return from_all(jnp.sum(from_all(chip, "wide", groups), axis=0), "narrow")


def local(test_matrix, weights, block_cols, export_rows, row_count):
    row_blocks, slots, size, _ = weights.shape
    columns, exports_each = test_matrix.shape[0], export_rows.shape[1]
    kernels = Kernels(columns, row_blocks, slots, size, exports_each, 9 * exports_each)
    part = lax.axis_index("wide") * lax.axis_size("narrow") + lax.axis_index("narrow")
    exports, slots_of = lax.dynamic_index_in_dim(export_rows, part, 0, keepdims=False), block_cols.T

    first_exports = kernels.export_first(exports, row_count, test_matrix, weights)
    before, after = along_narrow(first_exports)
    degree, live, first_input = kernels.first(row_count, test_matrix, weights)
    tables = (first_input, *halo_blocks(before, first_exports, after))
    second_exports = kernels.export_second(exports, slots_of, tables, degree, live, weights)
    before, after = along_narrow(second_exports)
    halo = halo_blocks(before, second_exports, after)
    second_input = kernels.second(slots_of, tables, degree, live, weights)
    sketch, gram = kernels.sketch(slots_of, second_input, halo, degree, live, weights)
    grams = gathered_grams(gram)
    node_total = lax.axis_size(AXES) * row_blocks * size
    return kernels.factor(math.sqrt(node_total), grams, sketch)


def solution(mesh):
    in_specs = (
        P(None, AXES),
        P(AXES, None, None, None),
        P(AXES, None),
        P(),
        P(AXES),
    )
    return jax.shard_map(local, mesh=mesh, in_specs=in_specs, out_specs=P(None, AXES), check_vma=False)
```

```python
import functools
import math

import jax
import jax.numpy as jnp
from jax import lax
from jax.experimental import pallas as pl
from jax.experimental.pallas import tpu as pltpu
from jax.sharding import PartitionSpec as P

EPSILON = 1e-06
AXES = ("wide", "narrow")
ROWS_STEP = 8
VMEM = pl.BlockSpec(memory_space=pltpu.VMEM)
LIMIT = 24 * 1024 * 1024
LAST = (((1,), (1,)), ((), ()))


def lanes(blocks):
    return jnp.concatenate([blocks[i] for i in range(blocks.shape[0])], axis=1)


def block_degree(blocks):
    ones = jnp.ones((8, blocks.shape[0] * blocks.shape[2]), blocks.dtype)
    sums = lax.dot_general(lanes(jnp.abs(blocks)), ones, LAST, preferred_element_type=jnp.float32)
    return sums.T[0:1] + EPSILON


def live_mask(row, block_size, present):
    position = lax.broadcasted_iota(jnp.int32, (1, block_size), 1) + row * block_size
    return (position < present).astype(jnp.float32)


def scaled(probe, degree, live):
    return (probe.astype(jnp.float32) * lax.rsqrt(degree) * live).astype(jnp.bfloat16)


def export_first_kernel(
    exports, count, probe, weights, out, probe_here, weights_here, probe_sems, weights_sems
):
    pieces = weights_sems.shape[1]
    slots, size = weights.shape[1] // pieces, weights.shape[2]
    rows = [exports[i] for i in range(exports.shape[0])]
    copies = []
    for i, row in enumerate(rows):
        start = pl.multiple_of(row * size, size)
        copies.append(pltpu.make_async_copy(probe.at[:, pl.ds(start, size)], probe_here.at[i], probe_sems.at[i]))
        for j in range(pieces):
            some = pl.ds(j * slots, slots)
            copies.append(
                pltpu.make_async_copy(weights.at[row, some], weights_here.at[i, some], weights_sems.at[i, j])
            )
    for copy in copies:
        copy.start()
    for copy in copies:
        copy.wait()
    for i, row in enumerate(rows):
        live = live_mask(row, size, count[0])
        out[i] = scaled(probe_here[i], block_degree(weights_here[i]), live)


def first_kernel(count, probe, weights, degree_out, live_out, out):
    rows, size = weights.shape[0], weights.shape[2]

    @pl.loop(0, rows // ROWS_STEP)
    def _(step):
        for i in range(ROWS_STEP):
            row = step * ROWS_STEP + i
            degree = block_degree(weights[row])
            degree_out[pl.ds(row, 1), :] = degree
            live = live_mask(row, size, count[0])
            live_out[pl.ds(row, 1), :] = live
            out[row] = scaled(probe[:, pl.ds(pl.multiple_of(row * size, size), size)], degree, live)


def fill_table(table, own, column, chip, other):
    start = own.shape[0]
    table[:start] = own[...]
    group = column.shape[0]
    odd = lax.axis_index("wide") & 1
    table[start + group : start + 2 * group] = column[...]
    table[pl.ds(start + 2 * group * (1 - odd), group)] = chip[...]
    table[pl.ds(start + 2 * group * odd, group)] = other[...]


def applied(table, slots, row, blocks):
    vectors = jnp.concatenate([table[slots[s, row]] for s in range(blocks.shape[0])], axis=1)
    return lax.dot_general(lanes(blocks), vectors, LAST, preferred_element_type=jnp.float32).T


def export_second_kernel(exports, slots, own, column, chip, other, degree, live, weights, out, table):
    fill_table(table, own, column, chip, other)
    for i in range(out.shape[0]):
        row = exports[i]
        product = applied(table, slots, row, weights[row])
        out[i] = (product / degree[pl.ds(row, 1), :] * live[pl.ds(row, 1), :]).astype(jnp.bfloat16)


def second_kernel(slots, own, column, chip, other, degree, live, weights, out, table):
    fill_table(table, own, column, chip, other)
    for row in range(out.shape[0]):
        product = applied(table, slots, row, weights[row])
        out[row] = (product / degree[row : row + 1, :] * live[row : row + 1, :]).astype(jnp.bfloat16)


def halves(value):
    high = value.astype(jnp.bfloat16)
    return high, (value - high.astype(jnp.float32)).astype(jnp.bfloat16)


def grid(size):
    shape = (size, size)
    return lax.broadcasted_iota(jnp.int32, shape, 0), lax.broadcasted_iota(jnp.int32, shape, 1)


def packed(square):
    half = square.shape[0] // 2
    down, along = grid(half)
    first, mixed, last = square[:half, :half], square[half:, :half], square[half:, half:]
    both = jnp.concatenate([mixed, jnp.where(down >= along, first, last)], axis=1)
    lines = jnp.concatenate([both[: half // 2], both[half // 2 :]], axis=1)
    diagonal = jnp.sum(jnp.where(down == along, last, 0.0), axis=0, keepdims=True)
    diagonal = jnp.concatenate([diagonal] * (lines.shape[1] // half), axis=1)
    return [lines[i : i + 1] for i in range(half // 2)] + [diagonal]


def unpacked(lines, diagonal):
    half = 2 * lines.shape[0]
    down, along = grid(half)
    both = jnp.concatenate([lines[:, : 2 * half], lines[:, 2 * half :]], axis=0)
    mixed, triangles = both[:, :half], both[:, half:]
    turned = triangles.T
    first = jnp.where(down >= along, triangles, turned)
    last = jnp.where(down < along, triangles, jnp.where(down > along, turned, diagonal[:, :half]))
    return jnp.concatenate(
        [jnp.concatenate([first, mixed.T], axis=1), jnp.concatenate([mixed, last], axis=1)], axis=0
    )


def sketch_kernel(slots, own, column, chip, other, degree, live, weights, sketch, gram, table):
    fill_table(table, own, column, chip, other)
    row_blocks, _, size, _ = weights.shape
    columns = table.shape[1]
    sums = jnp.zeros((2 * columns, columns), jnp.float32)
    for start in range(0, row_blocks, ROWS_STEP):
        for row in range(start, start + ROWS_STEP):
            product = applied(table, slots, row, weights[row])
            value = product * lax.rsqrt(degree[row : row + 1, :]) * live[row : row + 1, :]
            high, low = halves(value)
            sketch[:columns, row * size : (row + 1) * size] = high
            sketch[columns:, row * size : (row + 1) * size] = low
        some = slice(start * size, (start + ROWS_STEP) * size)
        sums = sums + lax.dot_general(
            sketch[:, some], sketch[:columns, some], LAST, preferred_element_type=jnp.float32
        )
    cross = sums[columns:]
    result = sums[:columns] + cross + cross.T
    for i, line in enumerate(packed(result)):
        gram[:, i * size : (i + 1) * size] = line


def factor_kernel(scale, grams, sketch, out, inverse, result, lines, sems):
    sums = grams[0]
    for i in range(1, grams.shape[0]):
        sums = sums + grams[i]
    size = lines.shape[1]
    for i in range(lines.shape[0]):
        lines[i : i + 1, :] = sums[:, i * size : (i + 1) * size]
    last = lines.shape[0] - 1
    total = unpacked(lines[:last], lines[last:])
    count = total.shape[0]
    down, along = grid(count)
    rest = jnp.concatenate([(down == along).astype(jnp.float32), total], axis=1)
    width = 16
    for start in range(0, count, width):
        sides = [
            jnp.broadcast_to(rest[:, count + start + j : count + start + j + 1], rest.shape) for j in range(width)
        ]
        below = lax.broadcasted_iota(jnp.int32, rest.shape, 0)
        for j in range(width):
            pivot = sides[j][j : j + 1, :]
            factors = jnp.where(below > j, sides[j] * (1.0 / pivot), 0.0)
            line = rest[j : j + 1, :]
            inverse[start + j : start + j + 1, :] = line * (lax.rsqrt(pivot) * scale)
            rest = rest - factors * line
            for k in range(j + 1, width):
                sides[k] = sides[k] - factors * sides[k][j : j + 1, :]
        if start + width < count:
            rest = rest[width:, :]
    high, low = halves(inverse[:, :count])
    factors = jnp.concatenate(
        [jnp.concatenate([high, high], axis=1), jnp.concatenate([low, jnp.zeros_like(low)], axis=1)], axis=0
    )
    pieces = sems.shape[0]
    length = result.shape[1] // pieces
    copies = []
    for i in range(pieces):
        some = slice(i * length, (i + 1) * length)
        both = jnp.dot(factors, sketch[:, some], preferred_element_type=jnp.float32)
        result[:, some] = both[:count] + both[count:]
        copies.append(pltpu.make_async_copy(result.at[:, some], out.at[:, some], sems.at[i]))
        copies[i].start()
    for copy in copies:
        copy.wait()


def cost(flops, moved):
    return pl.CostEstimate(flops=flops, bytes_accessed=moved, transcendentals=0)


SMEM = pl.BlockSpec(memory_space=pltpu.SMEM)
ANY = pl.BlockSpec(memory_space=pl.ANY)


def plain(kernel, in_specs, out_specs, out_shape, scratch, flops, moved):
    return pl.pallas_call(
        kernel,
        in_specs=in_specs,
        out_specs=out_specs,
        out_shape=out_shape,
        scratch_shapes=scratch,
        compiler_params=pltpu.CompilerParams(vmem_limit_bytes=LIMIT),
        cost_estimate=cost(flops, moved),
    )


def in_hbm(value):
    return pltpu.with_memory_space_constraint(value, pltpu.HBM)


class Kernels:
    def __init__(self, columns, row_blocks, slots, size, exports, halo):
        self.k, self.rb, self.nb, self.bs, self.eb = columns, row_blocks, slots, size, exports
        self.bytes_weights = row_blocks * slots * size * size * 2
        self.flops = 2 * columns * row_blocks * slots * size * size
        self.table = pltpu.VMEM((row_blocks + halo, columns, size), jnp.bfloat16)

    def export_first(self, exports, count, probe, weights):
        pieces = 4
        return plain(
            export_first_kernel,
            [SMEM, SMEM, ANY, ANY],
            VMEM,
            jax.ShapeDtypeStruct((self.eb, self.k, self.bs), jnp.bfloat16),
            [
                pltpu.VMEM((self.eb, self.k, self.bs), jnp.bfloat16),
                pltpu.VMEM((self.eb, self.nb, self.bs, self.bs), jnp.bfloat16),
                pltpu.SemaphoreType.DMA((self.eb,)),
                pltpu.SemaphoreType.DMA((self.eb, pieces)),
            ],
            self.flops // 16,
            self.bytes_weights // 16,
        )(exports, count, in_hbm(probe), in_hbm(weights))

    def first(self, count, probe, weights):
        return plain(
            first_kernel,
            [SMEM, VMEM, VMEM],
            [VMEM] * 3,
            [
                jax.ShapeDtypeStruct((self.rb, self.bs), jnp.float32),
                jax.ShapeDtypeStruct((self.rb, self.bs), jnp.float32),
                jax.ShapeDtypeStruct((self.rb, self.k, self.bs), jnp.bfloat16),
            ],
            [],
            self.flops,
            self.bytes_weights,
        )(count, probe, weights)

    def export_second(self, exports, slots, tables, degree, live, weights):
        return plain(
            export_second_kernel,
            [SMEM] * 2 + [VMEM] * 7,
            VMEM,
            jax.ShapeDtypeStruct((self.eb, self.k, self.bs), jnp.bfloat16),
            [self.table],
            self.flops // 16,
            self.bytes_weights // 16,
        )(exports, slots, *tables, degree, live, weights)

    def second(self, slots, tables, degree, live, weights):
        return plain(
            second_kernel,
            [SMEM] + [VMEM] * 7,
            VMEM,
            jax.ShapeDtypeStruct((self.rb, self.k, self.bs), jnp.bfloat16),
            [self.table],
            self.flops,
            self.bytes_weights,
        )(slots, *tables, degree, live, weights)

    def sketch(self, slots, own, halo, degree, live, weights):
        return plain(
            sketch_kernel,
            [SMEM] + [VMEM] * 7,
            [VMEM, VMEM],
            [
                jax.ShapeDtypeStruct((2 * self.k, self.rb * self.bs), jnp.bfloat16),
                jax.ShapeDtypeStruct((1, (self.k // 4 + 1) * self.bs), jnp.float32),
            ],
            [self.table],
            self.flops,
            self.bytes_weights,
        )(slots, own, *halo, degree, live, weights)

    def factor(self, scale, grams, sketch):
        shape = (self.k, sketch.shape[1])
        return plain(
            functools.partial(factor_kernel, scale),
            [VMEM, VMEM],
            ANY,
            jax.ShapeDtypeStruct(shape, jnp.float32),
            [
                pltpu.VMEM((self.k, 2 * self.k), jnp.float32),
                pltpu.VMEM(shape, jnp.float32),
                pltpu.VMEM((self.k // 4 + 1, self.bs), jnp.float32),
                pltpu.SemaphoreType.DMA((8,)),
            ],
            6 * self.k * sketch.size,
            4 * sketch.size,
        )(grams, sketch)


def shifted(value, axis, step):
    count = lax.axis_size(axis)
    return lax.ppermute(value, axis, [(i, (i + step) % count) for i in range(count)])


def swapped(value, axis, partner):
    return lax.ppermute(value, axis, [(i, partner(i)) for i in range(lax.axis_size(axis))])


def along_narrow(exports):
    return shifted(exports, "narrow", 1), shifted(exports, "narrow", -1)


def halo_blocks(before, exports, after):
    count = lax.axis_size("wide")
    column = jnp.concatenate([before, exports, after], axis=0)
    other = swapped(column, "wide", lambda i: (i + 1) % count if i % 2 else (i - 1) % count)
    chip = swapped(column, "wide", lambda i: i ^ 1)
    return column, chip, other


def from_all(value, axis, groups=None):
    count = len(groups[0]) if groups else lax.axis_size(axis)
    copies = jnp.broadcast_to(value[None], (count, *value.shape))
    return lax.all_to_all(copies, axis, 0, 0, axis_index_groups=groups, tiled=True)


def gathered_grams(gram):
    wide, narrow = lax.axis_size("wide"), lax.axis_size("narrow")
    groups = [list(range(core, wide, 2)) for core in range(2)]
    plane = jnp.sum(from_all(gram, "wide", groups), axis=0)
    lines = [[(2 * i + core) * narrow + j for core in range(2) for j in range(narrow)] for i in range(wide // 2)]
    return from_all(plane, AXES, lines)


def local(test_matrix, weights, block_cols, export_rows, row_count):
    row_blocks, slots, size, _ = weights.shape
    columns, exports_each = test_matrix.shape[0], export_rows.shape[1]
    kernels = Kernels(columns, row_blocks, slots, size, exports_each, 9 * exports_each)
    part = lax.axis_index("wide") * lax.axis_size("narrow") + lax.axis_index("narrow")
    exports, slots_of = lax.dynamic_index_in_dim(export_rows, part, 0, keepdims=False), block_cols.T

    first_exports = kernels.export_first(exports, row_count, test_matrix, weights)
    before, after = along_narrow(first_exports)
    degree, live, first_input = kernels.first(row_count, test_matrix, weights)
    tables = (first_input, *halo_blocks(before, first_exports, after))
    second_exports = kernels.export_second(exports, slots_of, tables, degree, live, weights)
    before, after = along_narrow(second_exports)
    halo = halo_blocks(before, second_exports, after)
    second_input = kernels.second(slots_of, tables, degree, live, weights)
    sketch, gram = kernels.sketch(slots_of, second_input, halo, degree, live, weights)
    grams = gathered_grams(gram)
    node_total = lax.axis_size(AXES) * row_blocks * size
    return kernels.factor(math.sqrt(node_total), grams, sketch)


def solution(mesh):
    in_specs = (
        P(None, AXES),
        P(AXES, None, None, None),
        P(AXES, None),
        P(),
        P(AXES),
    )
    return jax.shard_map(local, mesh=mesh, in_specs=in_specs, out_specs=P(None, AXES), check_vma=False)
```

```python
import functools
import math

import jax
import jax.numpy as jnp
from jax import lax
from jax.experimental import pallas as pl
from jax.experimental.pallas import tpu as pltpu
from jax.sharding import PartitionSpec as P

EPSILON = 1e-06
AXES = ("wide", "narrow")
ROWS_STEP = 8
VMEM = pl.BlockSpec(memory_space=pltpu.VMEM)
LIMIT = 24 * 1024 * 1024
LAST = (((1,), (1,)), ((), ()))


def lanes(blocks):
    return jnp.concatenate([blocks[i] for i in range(blocks.shape[0])], axis=1)


def block_degree(blocks):
    ones = jnp.ones((8, blocks.shape[0] * blocks.shape[2]), blocks.dtype)
    sums = lax.dot_general(lanes(jnp.abs(blocks)), ones, LAST, preferred_element_type=jnp.float32)
    return sums.T[0:1] + EPSILON


def live_mask(row, block_size, present):
    position = lax.broadcasted_iota(jnp.int32, (1, block_size), 1) + row * block_size
    return (position < present).astype(jnp.float32)


def scaled(probe, degree, live):
    return (probe.astype(jnp.float32) * lax.rsqrt(degree) * live).astype(jnp.bfloat16)


def export_first_kernel(
    exports, count, probe, weights, out, probe_here, weights_here, probe_sems, weights_sems
):
    pieces = weights_sems.shape[1]
    slots, size = weights.shape[1] // pieces, weights.shape[2]
    rows = [exports[i] for i in range(exports.shape[0])]
    copies = []
    for i, row in enumerate(rows):
        start = pl.multiple_of(row * size, size)
        copies.append(pltpu.make_async_copy(probe.at[:, pl.ds(start, size)], probe_here.at[i], probe_sems.at[i]))
        for j in range(pieces):
            some = pl.ds(j * slots, slots)
            copies.append(
                pltpu.make_async_copy(weights.at[row, some], weights_here.at[i, some], weights_sems.at[i, j])
            )
    for copy in copies:
        copy.start()
    for copy in copies:
        copy.wait()
    for i, row in enumerate(rows):
        live = live_mask(row, size, count[0])
        out[i] = scaled(probe_here[i], block_degree(weights_here[i]), live)


def first_kernel(count, probe, weights, degree_out, live_out, out):
    rows, size = weights.shape[0], weights.shape[2]

    for row in range(rows):
        degree = block_degree(weights[row])
        degree_out[row : row + 1, :] = degree
        live = live_mask(row, size, count[0])
        live_out[row : row + 1, :] = live
        out[row] = scaled(probe[:, row * size : (row + 1) * size], degree, live)


def fill_table(table, own, column, chip, other):
    start = own.shape[0]
    table[:start] = own[...]
    group = column.shape[0]
    each = group // 3
    odd, narrow_odd = lax.axis_index("wide") & 1, lax.axis_index("narrow") & 1
    sources = ((column, group), (chip, 2 * group * (1 - odd)), (other, 2 * group * odd))
    for source, place in sources:
        place = start + place
        table[pl.ds(place + 2 * each * (1 - narrow_odd), each)] = source[:each]
        table[pl.ds(place + each, each)] = source[each : 2 * each]
        table[pl.ds(place + 2 * each * narrow_odd, each)] = source[2 * each :]


def applied(table, slots, row, blocks):
    vectors = jnp.concatenate([table[slots[s, row]] for s in range(blocks.shape[0])], axis=1)
    return lax.dot_general(lanes(blocks), vectors, LAST, preferred_element_type=jnp.float32).T


def export_second_kernel(exports, slots, own, column, chip, other, degree, live, weights, out, table):
    fill_table(table, own, column, chip, other)
    for i in range(out.shape[0]):
        row = exports[i]
        product = applied(table, slots, row, weights[row])
        out[i] = (product / degree[pl.ds(row, 1), :] * live[pl.ds(row, 1), :]).astype(jnp.bfloat16)


def second_kernel(slots, own, column, chip, other, degree, live, weights, out, table):
    fill_table(table, own, column, chip, other)
    for row in range(out.shape[0]):
        product = applied(table, slots, row, weights[row])
        out[row] = (product / degree[row : row + 1, :] * live[row : row + 1, :]).astype(jnp.bfloat16)


def halves(value):
    high = value.astype(jnp.bfloat16)
    return high, (value - high.astype(jnp.float32)).astype(jnp.bfloat16)


def grid(size):
    shape = (size, size)
    return lax.broadcasted_iota(jnp.int32, shape, 0), lax.broadcasted_iota(jnp.int32, shape, 1)


def packed(square):
    half = square.shape[0] // 2
    down, along = grid(half)
    first, mixed, last = square[:half, :half], square[half:, :half], square[half:, half:]
    both = jnp.concatenate([mixed, jnp.where(down >= along, first, last)], axis=1)
    lines = jnp.concatenate([both[: half // 2], both[half // 2 :]], axis=1)
    diagonal = jnp.sum(jnp.where(down == along, last, 0.0), axis=0, keepdims=True)
    diagonal = jnp.concatenate([diagonal] * (lines.shape[1] // half), axis=1)
    return [lines[i : i + 1] for i in range(half // 2)] + [diagonal]


def unpacked(lines, diagonal):
    half = 2 * lines.shape[0]
    down, along = grid(half)
    both = jnp.concatenate([lines[:, : 2 * half], lines[:, 2 * half :]], axis=0)
    mixed, triangles = both[:, :half], both[:, half:]
    turned = triangles.T
    first = jnp.where(down >= along, triangles, turned)
    last = jnp.where(down < along, triangles, jnp.where(down > along, turned, diagonal[:, :half]))
    return jnp.concatenate(
        [jnp.concatenate([first, mixed.T], axis=1), jnp.concatenate([mixed, last], axis=1)], axis=0
    )


def sketch_kernel(slots, own, column, chip, other, degree, live, weights, sketch, gram, table):
    fill_table(table, own, column, chip, other)
    row_blocks, _, size, _ = weights.shape
    columns = table.shape[1]
    sums = jnp.zeros((2 * columns, columns), jnp.float32)
    for start in range(0, row_blocks, ROWS_STEP):
        for row in range(start, start + ROWS_STEP):
            product = applied(table, slots, row, weights[row])
            value = product * lax.rsqrt(degree[row : row + 1, :]) * live[row : row + 1, :]
            high, low = halves(value)
            sketch[:columns, row * size : (row + 1) * size] = high
            sketch[columns:, row * size : (row + 1) * size] = low
        some = slice(start * size, (start + ROWS_STEP) * size)
        sums = sums + lax.dot_general(
            sketch[:, some], sketch[:columns, some], LAST, preferred_element_type=jnp.float32
        )
    cross = sums[columns:]
    result = sums[:columns] + cross + cross.T
    for i, line in enumerate(packed(result)):
        gram[:, i * size : (i + 1) * size] = line


def factor_kernel(scale, grams, sketch, out, inverse, result, lines, sems):
    sums = grams[0]
    for i in range(1, grams.shape[0]):
        sums = sums + grams[i]
    size = lines.shape[1]
    for i in range(lines.shape[0]):
        lines[i : i + 1, :] = sums[:, i * size : (i + 1) * size]
    last = lines.shape[0] - 1
    total = unpacked(lines[:last], lines[last:])
    count = total.shape[0]
    down, along = grid(count)
    rest = jnp.concatenate([(down == along).astype(jnp.float32), total], axis=1)
    width = 16
    for start in range(0, count, width):
        sides = [
            jnp.broadcast_to(rest[:, count + start + j : count + start + j + 1], rest.shape) for j in range(width)
        ]
        below = lax.broadcasted_iota(jnp.int32, rest.shape, 0)
        for j in range(width):
            pivot = sides[j][j : j + 1, :]
            factors = jnp.where(below > j, sides[j] * (1.0 / pivot), 0.0)
            line = rest[j : j + 1, :]
            inverse[start + j : start + j + 1, :] = line * (lax.rsqrt(pivot) * scale)
            rest = rest - factors * line
            for k in range(j + 1, width):
                sides[k] = sides[k] - factors * sides[k][j : j + 1, :]
        if start + width < count:
            rest = rest[width:, :]
    high, low = halves(inverse[:, :count])
    factors = jnp.concatenate(
        [jnp.concatenate([high, high], axis=1), jnp.concatenate([low, jnp.zeros_like(low)], axis=1)], axis=0
    )
    pieces = sems.shape[0]
    length = result.shape[1] // pieces
    copies = []
    for i in range(pieces):
        some = slice(i * length, (i + 1) * length)
        both = jnp.dot(factors, sketch[:, some], preferred_element_type=jnp.float32)
        result[:, some] = both[:count] + both[count:]
        copies.append(pltpu.make_async_copy(result.at[:, some], out.at[:, some], sems.at[i]))
        copies[i].start()
    for copy in copies:
        copy.wait()


def cost(flops, moved):
    return pl.CostEstimate(flops=flops, bytes_accessed=moved, transcendentals=0)


SMEM = pl.BlockSpec(memory_space=pltpu.SMEM)
ANY = pl.BlockSpec(memory_space=pl.ANY)


def plain(kernel, in_specs, out_specs, out_shape, scratch, flops, moved):
    return pl.pallas_call(
        kernel,
        in_specs=in_specs,
        out_specs=out_specs,
        out_shape=out_shape,
        scratch_shapes=scratch,
        compiler_params=pltpu.CompilerParams(vmem_limit_bytes=LIMIT),
        cost_estimate=cost(flops, moved),
    )


def in_hbm(value):
    return pltpu.with_memory_space_constraint(value, pltpu.HBM)


class Kernels:
    def __init__(self, columns, row_blocks, slots, size, exports, halo):
        self.k, self.rb, self.nb, self.bs, self.eb = columns, row_blocks, slots, size, exports
        self.bytes_weights = row_blocks * slots * size * size * 2
        self.flops = 2 * columns * row_blocks * slots * size * size
        self.table = pltpu.VMEM((row_blocks + halo, columns, size), jnp.bfloat16)

    def export_first(self, exports, count, probe, weights):
        pieces = 1
        return plain(
            export_first_kernel,
            [SMEM, SMEM, ANY, ANY],
            VMEM,
            jax.ShapeDtypeStruct((self.eb, self.k, self.bs), jnp.bfloat16),
            [
                pltpu.VMEM((self.eb, self.k, self.bs), jnp.bfloat16),
                pltpu.VMEM((self.eb, self.nb, self.bs, self.bs), jnp.bfloat16),
                pltpu.SemaphoreType.DMA((self.eb,)),
                pltpu.SemaphoreType.DMA((self.eb, pieces)),
            ],
            self.flops // 16,
            self.bytes_weights // 16,
        )(exports, count, in_hbm(probe), in_hbm(weights))

    def first(self, count, probe, weights):
        return plain(
            first_kernel,
            [SMEM, VMEM, VMEM],
            [VMEM] * 3,
            [
                jax.ShapeDtypeStruct((self.rb, self.bs), jnp.float32),
                jax.ShapeDtypeStruct((self.rb, self.bs), jnp.float32),
                jax.ShapeDtypeStruct((self.rb, self.k, self.bs), jnp.bfloat16),
            ],
            [],
            self.flops,
            self.bytes_weights,
        )(count, probe, weights)

    def export_second(self, exports, slots, tables, degree, live, weights):
        return plain(
            export_second_kernel,
            [SMEM] * 2 + [VMEM] * 7,
            VMEM,
            jax.ShapeDtypeStruct((self.eb, self.k, self.bs), jnp.bfloat16),
            [self.table],
            self.flops // 16,
            self.bytes_weights // 16,
        )(exports, slots, *tables, degree, live, weights)

    def second(self, slots, tables, degree, live, weights):
        return plain(
            second_kernel,
            [SMEM] + [VMEM] * 7,
            VMEM,
            jax.ShapeDtypeStruct((self.rb, self.k, self.bs), jnp.bfloat16),
            [self.table],
            self.flops,
            self.bytes_weights,
        )(slots, *tables, degree, live, weights)

    def sketch(self, slots, own, halo, degree, live, weights):
        return plain(
            sketch_kernel,
            [SMEM] + [VMEM] * 7,
            [VMEM, VMEM],
            [
                jax.ShapeDtypeStruct((2 * self.k, self.rb * self.bs), jnp.bfloat16),
                jax.ShapeDtypeStruct((1, (self.k // 4 + 1) * self.bs), jnp.float32),
            ],
            [self.table],
            self.flops,
            self.bytes_weights,
        )(slots, own, *halo, degree, live, weights)

    def factor(self, scale, grams, sketch):
        shape = (self.k, sketch.shape[1])
        return plain(
            functools.partial(factor_kernel, scale),
            [VMEM, VMEM],
            ANY,
            jax.ShapeDtypeStruct(shape, jnp.float32),
            [
                pltpu.VMEM((self.k, 2 * self.k), jnp.float32),
                pltpu.VMEM(shape, jnp.float32),
                pltpu.VMEM((self.k // 4 + 1, self.bs), jnp.float32),
                pltpu.SemaphoreType.DMA((8,)),
            ],
            6 * self.k * sketch.size,
            4 * sketch.size,
        )(grams, sketch)


def swapped(value, axis, partner):
    return lax.ppermute(value, axis, [(i, partner(i)) for i in range(lax.axis_size(axis))])


def along_narrow(exports):
    count = lax.axis_size("narrow")
    near = swapped(exports, "narrow", lambda i: i ^ 1)
    far = swapped(exports, "narrow", lambda i: (i + 1) % count if i % 2 else (i - 1) % count)
    return near, far


def halo_blocks(before, exports, after):
    count = lax.axis_size("wide")
    column = jnp.concatenate([before, exports, after], axis=0)
    other = swapped(column, "wide", lambda i: (i + 1) % count if i % 2 else (i - 1) % count)
    chip = swapped(column, "wide", lambda i: i ^ 1)
    return column, chip, other


def from_all(value, axis, groups=None):
    count = len(groups[0]) if groups else lax.axis_size(axis)
    copies = jnp.broadcast_to(value[None], (count, *value.shape))
    return lax.all_to_all(copies, axis, 0, 0, axis_index_groups=groups, tiled=True)


def gathered_grams(gram):
    chip = gram + swapped(gram, "wide", lambda i: i ^ 1)
    count = lax.axis_size("wide")
    groups = [list(range(core, count, 2)) for core in range(2)]
    return from_all(jnp.sum(from_all(chip, "wide", groups), axis=0), "narrow")


def local(test_matrix, weights, block_cols, export_rows, row_count):
    row_blocks, slots, size, _ = weights.shape
    columns, exports_each = test_matrix.shape[0], export_rows.shape[1]
    kernels = Kernels(columns, row_blocks, slots, size, exports_each, 9 * exports_each)
    part = lax.axis_index("wide") * lax.axis_size("narrow") + lax.axis_index("narrow")
    exports, slots_of = lax.dynamic_index_in_dim(export_rows, part, 0, keepdims=False), block_cols.T

    first_exports = kernels.export_first(exports, row_count, test_matrix, weights)
    before, after = along_narrow(first_exports)
    degree, live, first_input = kernels.first(row_count, test_matrix, weights)
    tables = (first_input, *halo_blocks(before, first_exports, after))
    second_exports = kernels.export_second(exports, slots_of, tables, degree, live, weights)
    before, after = along_narrow(second_exports)
    halo = halo_blocks(before, second_exports, after)
    second_input = kernels.second(slots_of, tables, degree, live, weights)
    sketch, gram = kernels.sketch(slots_of, second_input, halo, degree, live, weights)
    grams = gathered_grams(gram)
    node_total = lax.axis_size(AXES) * row_blocks * size
    return kernels.factor(math.sqrt(node_total), grams, sketch)


def solution(mesh):
    in_specs = (
        P(None, AXES),
        P(AXES, None, None, None),
        P(AXES, None),
        P(),
        P(AXES),
    )
    return jax.shard_map(local, mesh=mesh, in_specs=in_specs, out_specs=P(None, AXES), check_vma=False)
```
